512 devices in a mesh: ctx: 32 (over x, z_lo), tp: 4 (over z_hi, core), dp: 4 (over y).
Axes of the slice: x: 4, y: 4, z: 16 (z_hi: 2, z_lo: 8; z = z_hi * 8 + z_lo), core: 2. Of those that a mesh axis runs over, the one named last changes fastest.
Arguments:
- queries: bfloat16 [32768, 4096], P(('dp', 'ctx'), 'tp'), parts along dimension 0, may hold values from -10 to 10
- keys: bfloat16 [32768, 512], P(('dp', 'ctx'), 'tp'), parts along dimension 0, may hold values from -4 to 4
- values: bfloat16 [32768, 512], P(('dp', 'ctx'), 'tp'), parts along dimension 0, may hold values from -5 to 5
- doc_ids: int32 [32768], P(('dp', 'ctx')), parts along dimension 0, may hold values from 0 to 127, never falling along the last dimension, each value on 1 to 4096 neighbouring positions
Outputs:
- attended: bfloat16 [32768, 4096], P(('dp', 'ctx'), 'tp'), parts along dimension 0
The draws below stay inside these ranges and needn't reach their ends.
There are 4 independent parts, one for each index of `dp`. The reference program is written for one: setup_inputs(seed, part) draws one part's arguments, and reference() takes and returns one part's arrays. A program takes and returns all parts, laid end to end along the dimension named above; each array names one. Nothing has to cross between parts.
Inputs may be any that keep to these rules, and one draw needn't show every extreme that they name: `doc_ids`: document numbers never fall along the sequence, every number appears, and no document is longer than 4096 positions; one has exactly 4096.
All inputs are finite; a program needn't handle non-finite values.
Results may differ from the reference program's by a relative error of at most 0.003.
Values may be sent and summed in bfloat16 or wider, within the bound.
No kernel may reach another device: no remote copies, remote signals or barrier semaphores. Data moves between devices by JAX's collectives and lax.ppermute only.
A program may use at most 64 MiB of HBM per device.

```python
import math
import jax
import jax.numpy as jnp
import numpy as np
from jax import lax

QUERY_HEADS = 32
KEY_VALUE_HEADS = 4
HEAD_SIZE = 128
PACKED_LENGTH = 8192
LONGEST = 4096
DOCS = 128


def shared_keys(key):
    base_offset = jnp.clip(jax.random.normal(jax.random.fold_in(key, 101), (PACKED_LENGTH, KEY_VALUE_HEADS * HEAD_SIZE), jnp.float32), -4.0, 4.0)
    return base_offset


def draw_keys(key, part):
    base_offset = shared_keys(key)
    result = base_offset
    return result.astype(jnp.bfloat16)


def draw_queries(key, part):
    key = jax.random.fold_in(key, 5)
    result = jnp.clip(jax.random.normal(key, (PACKED_LENGTH, QUERY_HEADS * HEAD_SIZE), jnp.float32), -4.0, 4.0)
    return result.astype(jnp.bfloat16)


def levels(rng, shape, cuts, smallest, top_value):
    def one(axis_at, blocks):
        draws = jax.random.uniform(jax.random.fold_in(jax.random.fold_in(rng, 6), axis_at), (blocks,), jnp.float32, smallest / len(cuts), top_value / len(cuts))
        return jnp.repeat(jnp.exp(draws), shape[axis_at] // blocks).reshape((-1,) + (1,) * (len(shape) - axis_at - 1))

    level = one(*cuts[0])
    for cut in cuts[1:]:
        level = level * one(*cut)
    return level


def profile(count, total, most, skew):
    portions = [(1 << 20) // math.isqrt(standing ** skew) + 1 for standing in range(2, count + 1)]
    rest, given = total - most - (count - 1), [1] * (count - 1)
    while rest > 0:
        movable = [i for i in range(count - 1) if given[i] < most]
        mass, left = sum([portions[i] for i in movable]), rest
        for i in movable:
            addition = min(most - given[i], max(1, left * portions[i] // mass), rest)
            given[i] = given[i] + addition
            rest = rest - addition
    return np.array([most] + given)


def uneven_parts(own_key, count, total, most, lean):
    if count == 2:
        one = jax.random.randint(own_key, (), max(1, total - most), min(most, total - 1) + 1)
        return jnp.stack([one, total - one])
    sizes = jnp.asarray(profile(count, total, most, lean), jnp.int32)
    twos = (count - 1) // 2
    giver, receiver = sizes[1:1 + 2 * twos:2], sizes[2:2 + 2 * twos:2]
    room = jnp.minimum(giver - 1, most - receiver)
    passed = jax.random.randint(jax.random.fold_in(own_key, 1), (twos,), 0, 1 << 20) % (room + 1)
    sizes = sizes.at[1:1 + 2 * twos:2].set(giver - passed).at[2:2 + 2 * twos:2].set(receiver + passed)
    return sizes[jax.random.permutation(jax.random.fold_in(own_key, 2), count)]


def normal_values(key, shape, spread, most, cuts=(), kind=jnp.bfloat16):
    values = spread * jax.random.normal(key, shape, jnp.float32)
    if cuts:
        values = values * levels(key, shape, cuts, -0.22, 0.18)
    return jnp.clip(values, -most, most).astype(kind)


def setup_inputs(seed: int = 0, part: int = 0) -> dict:
    seeds = jax.random.split(jax.random.key(seed), 5)
    part_keys = jax.random.split(jax.random.fold_in(seeds[4], part), 5)
    return {
        "queries": draw_queries(jax.random.fold_in(jax.random.fold_in(seeds[4], part), 71), part),
        "keys": draw_keys(jax.random.fold_in(jax.random.fold_in(seeds[4], part), 71), part),
        "values": normal_values(part_keys[2], (PACKED_LENGTH, KEY_VALUE_HEADS * HEAD_SIZE), 1.0, 5.0, ((0, 32), (1, 4))),
        "doc_ids": jnp.searchsorted(jnp.cumsum(uneven_parts(part_keys[3], DOCS, PACKED_LENGTH, LONGEST, 2)), jnp.arange(PACKED_LENGTH), side="right").astype(jnp.int32),
    }


NEGATIVE = -1.0e30


def reference(queries, keys, values, doc_ids):
    total_count = queries.shape[0]
    queries_per_group = QUERY_HEADS // KEY_VALUE_HEADS
    block_rows = math.gcd(total_count, 512)
    width = min(total_count, LONGEST + block_rows)
    scale = HEAD_SIZE ** -0.5
    grouped_queries = queries.reshape(total_count, KEY_VALUE_HEADS, queries_per_group, HEAD_SIZE)
    grouped_key_rows = keys.reshape(total_count, KEY_VALUE_HEADS, HEAD_SIZE)
    grouped_value_rows = values.reshape(total_count, KEY_VALUE_HEADS, HEAD_SIZE)

    def one_block(number):
        first = (number * block_rows).astype(jnp.int32)
        key_first = jnp.clip(first + block_rows - width, 0, total_count - width).astype(jnp.int32)
        query_block = lax.dynamic_slice_in_dim(grouped_queries, first, block_rows, 0).astype(jnp.float32)
        key_block = lax.dynamic_slice_in_dim(grouped_key_rows, key_first, width, 0).astype(jnp.float32)
        value_block = lax.dynamic_slice_in_dim(grouped_value_rows, key_first, width, 0).astype(jnp.float32)
        scores = jnp.einsum("qhgd,khd->qhgk", query_block, key_block, precision=lax.Precision.HIGHEST) * scale
        query_ids = lax.dynamic_slice_in_dim(doc_ids, first, block_rows, 0)
        key_ids = lax.dynamic_slice_in_dim(doc_ids, key_first, width, 0)
        query_pos = first + jnp.arange(block_rows, dtype=jnp.int32)
        key_pos = key_first + jnp.arange(width, dtype=jnp.int32)
        visible = (query_ids[:, None] == key_ids[None, :]) & (key_pos[None, :] <= query_pos[:, None])
        visible = visible[:, None, None, :]
        row_max = jnp.max(jnp.where(visible, scores, NEGATIVE), axis=-1, keepdims=True)
        weights = jnp.where(visible, jnp.exp(scores - row_max), 0.0)
        weight_sum = jnp.sum(weights, axis=-1)
        rounded = lax.optimization_barrier(weights.astype(jnp.bfloat16)).astype(jnp.float32)
        mixed = jnp.einsum("qhgk,khd->qhgd", rounded, value_block, precision=lax.Precision.HIGHEST)
        mixed = mixed / weight_sum[..., None]
        return mixed.reshape(block_rows, QUERY_HEADS * HEAD_SIZE).astype(jnp.bfloat16)

    blocks = lax.map(one_block, jnp.arange(total_count // block_rows, dtype=jnp.int32))
    return blocks.reshape(total_count, QUERY_HEADS * HEAD_SIZE)
```

```python
import functools
import math

import jax
import jax.numpy as jnp
from jax import lax
from jax.experimental import pallas as pl
from jax.experimental.pallas import tpu as pltpu
from jax.sharding import PartitionSpec as P

HEAD = 128
BLOCK = 256
HEADS = 8
IDS = 16
SLOT = 2 * BLOCK + IDS
NEGATIVE = -1e30
FACTOR = HEAD**-0.5 * math.log2(math.e)
NX, NZ = 4, 8


def contract_last(a, b):
    return lax.dot_general(a, b, (((1,), (1,)), ((), ())), preferred_element_type=jnp.float32)


def own_kernel(q_ref, own_ref, m_ref, l_ref, acc_ref):
    ids = own_ref[2 * BLOCK :, :].astype(jnp.float32)
    row = jnp.concatenate([ids[0:1, :], ids[1:2, :]], axis=1)
    key_ids = jnp.broadcast_to(row, (BLOCK, BLOCK))
    query_ids = key_ids.T
    q_pos = lax.broadcasted_iota(jnp.int32, (BLOCK, BLOCK), 0)
    k_pos = lax.broadcasted_iota(jnp.int32, (BLOCK, BLOCK), 1)
    visible = (key_ids == query_ids) & (k_pos <= q_pos)
    in_first = (query_ids == key_ids[0:1, 0:1])[:, :HEAD]
    keys = own_ref[:BLOCK, :]
    values = own_ref[BLOCK : 2 * BLOCK, :]
    for h in range(HEADS):
        rows = pl.ds(h * BLOCK, BLOCK)
        scores = contract_last(q_ref[:, h * HEAD : (h + 1) * HEAD], keys) * FACTOR
        scores = jnp.where(visible, scores, NEGATIVE)
        top = jnp.max(scores, axis=1, keepdims=True)
        weights = jnp.exp2(scores - top)
        l_ref[rows, :] = weights[:, :HEAD] + weights[:, HEAD:]
        acc_ref[rows, :] = jnp.dot(
            weights.astype(jnp.bfloat16), values, preferred_element_type=jnp.float32
        )
        m_ref[rows, :] = jnp.where(in_first, jnp.broadcast_to(top, (BLOCK, HEAD)), -NEGATIVE)


def more_kernel(counts, last, *refs):
    n = len(counts)
    ok_ref, q_ref, own_ref, m_in, l_in, acc_in = refs[:6]
    slots = refs[6 : 6 + n]
    if last:
        out_ref, m_ref, l_ref, acc_ref = refs[6 + n :]
    else:
        m_ref, l_ref, acc_ref = refs[6 + n :]
    m_ref[...] = m_in[...]
    l_ref[...] = l_in[...]
    acc_ref[...] = acc_in[...]
    first_id = own_ref[2 * BLOCK :, :].astype(jnp.float32)[0:1, 0:1]
    at = 0
    for ref, count in zip(slots, counts):
        for k in range(count):
            base = k * SLOT
            ids = ref[base + 2 * BLOCK : base + SLOT, :].astype(jnp.float32)
            seen = jnp.sum(jnp.where(ids == first_id, 1.0, 0.0)).astype(jnp.int32)
            seen = seen * ok_ref[at]
            at += 1

            @pl.when(seen > 0)
            def _():
                k_pos = lax.broadcasted_iota(jnp.int32, (1, BLOCK), 1)
                bias = jnp.where(k_pos >= BLOCK - seen, 0.0, NEGATIVE)
                keys = ref[base : base + BLOCK, :]
                values = ref[base + BLOCK : base + 2 * BLOCK, :]

                def head(h, carry):
                    rows = pl.ds(pl.multiple_of(h * BLOCK, BLOCK), BLOCK)
                    q = q_ref[:, pl.ds(pl.multiple_of(h * HEAD, HEAD), HEAD)]
                    scores = contract_last(q, keys) * FACTOR + bias
                    old = m_ref[rows, :]
                    new = jnp.maximum(old, jnp.max(scores, axis=1, keepdims=True))
                    fade = jnp.exp2(old - new)
                    weights = jnp.exp2(scores - new[:, 0:1])
                    l_ref[rows, :] = l_ref[rows, :] * fade + weights[:, :HEAD] + weights[:, HEAD:]
                    acc_ref[rows, :] = acc_ref[rows, :] * fade + jnp.dot(
                        weights.astype(jnp.bfloat16), values, preferred_element_type=jnp.float32
                    )
                    m_ref[rows, :] = new
                    return carry

                lax.fori_loop(0, HEADS, head, 0, unroll=4)

    if last:
        for h in range(HEADS):
            rows = pl.ds(h * BLOCK, BLOCK)
            total = jnp.sum(l_ref[rows, :], axis=1, keepdims=True)
            out_ref[:, h * HEAD : (h + 1) * HEAD] = (acc_ref[rows, :] / total).astype(jnp.bfloat16)


VMEM = pl.BlockSpec(memory_space=pltpu.VMEM)
SMEM = pl.BlockSpec(memory_space=pltpu.SMEM)
STATE = [jax.ShapeDtypeStruct((HEADS * BLOCK, HEAD), jnp.float32)] * 3
PARAMS = pltpu.CompilerParams(vmem_limit_bytes=40 * 1024 * 1024)


def cost(blocks):
    pairs = blocks * HEADS * BLOCK * BLOCK
    return pl.CostEstimate(
        flops=4 * HEAD * pairs, bytes_accessed=4 * 2**20, transcendentals=pairs
    )


def attend_own(q, own):
    return pl.pallas_call(
        own_kernel, out_shape=STATE, in_specs=[VMEM] * 2, out_specs=[VMEM] * 3,
        compiler_params=PARAMS, cost_estimate=cost(1), name="attend_own",
    )(q, own)


def attend_more(state, q, own, arrays, ok, last=False):
    counts = [a.shape[0] // SLOT for a in arrays]
    ok = jnp.stack([jnp.asarray(o, jnp.int32) for o in ok])
    scratch = [pltpu.VMEM((HEADS * BLOCK, HEAD), jnp.float32)] * 3 if last else []
    out = jax.ShapeDtypeStruct((BLOCK, HEADS * HEAD), jnp.bfloat16)
    return pl.pallas_call(
        functools.partial(more_kernel, counts, last),
        out_shape=out if last else STATE,
        in_specs=[SMEM] + [VMEM] * (5 + len(arrays)),
        out_specs=VMEM if last else [VMEM] * 3,
        scratch_shapes=scratch,
        compiler_params=PARAMS, cost_estimate=cost(sum(counts)),
        name="attend_last" if last else "attend_more",
    )(ok, q, own, *state, *arrays)


def exchange(v, mask):
    return lax.ppermute(v, "ctx", [(i, i ^ mask) for i in range(NX * NZ)])


def along_x(v, steps):
    return lax.ppermute(v, "ctx", [(i, i + NZ * steps) for i in range((NX - steps) * NZ)])


def per_device(queries, keys, values, doc_ids):
    index = lax.axis_index("ctx")
    z = index % NZ
    bit = [(z >> b) & 1 for b in range(3)]
    one = jnp.int32(1)
    ids = (doc_ids + 1).astype(jnp.bfloat16).reshape(2, HEAD)
    ids = jnp.pad(ids, ((0, IDS - 2), (0, 0)))
    own = jnp.concatenate([keys, values, ids], axis=0)

    def hold(*values):
        return lax.optimization_barrier(values)

    p1 = exchange(own, 4)
    b0 = along_x(own, 1)
    c0 = along_x(own, 2)
    state = attend_own(queries, own)
    p1, b0, c0, state = hold(p1, b0, c0, state)
    p2 = exchange(jnp.concatenate([own, p1]), 2)
    near0 = exchange(jnp.concatenate([b0, jnp.where(bit[0] == 0, own, c0)]), 1)
    b1 = along_x(p1, 1)
    c1 = along_x(p1, 2)
    state = attend_more(state, queries, own, [p1, b0, c0], [bit[2], one, one])
    p2, near0, b1, c1, state = hold(p2, near0, b1, c1, state)
    near1 = exchange(jnp.concatenate([b1, jnp.where(bit[2] == 1, p1, c1), p2]), 1)
    b2 = along_x(p2, 1)
    c2 = along_x(p2, 2)
    state = attend_more(
        state, queries, own, [p2, near0, b1, c1], [bit[1], bit[2], one, one, one, one]
    )
    near1, b2, c2, state = hold(near1, b2, c2, state)
    c3 = exchange(c2, 1)
    b3 = along_x(near1[2 * SLOT :], 1)
    state = attend_more(
        state, queries, own, [near1, b2, c2], [one, one, bit[1], bit[2], one, one, one, one]
    )
    c3, b3, state = hold(c3, b3, state)
    return attend_more(state, queries, own, [c3, b3], [one] * 4, last=True)


def solution(mesh):
    return jax.shard_map(
        per_device,
        mesh=mesh,
        in_specs=(
            P(("dp", "ctx"), "tp"),
            P(("dp", "ctx"), "tp"),
            P(("dp", "ctx"), "tp"),
            P(("dp", "ctx")),
        ),
        out_specs=P(("dp", "ctx"), "tp"),
        check_vma=False,
    )
```

```python
import functools
import math

import jax
import jax.numpy as jnp
from jax import lax
from jax.experimental import pallas as pl
from jax.experimental.pallas import tpu as pltpu
from jax.sharding import PartitionSpec as P

HEAD = 128
BLOCK = 256
HEADS = 8
TOGETHER = 4
IDS = 16
SLOT = 2 * BLOCK + IDS
WIDE = 2 * BLOCK
NX, NZ = 4, 8
NEGATIVE = -1e30
FACTOR = HEAD**-0.5 * math.log2(math.e)
LOW, HIGH = 2.0**-80, 2.0**100


def contract_last(a, b):
    return lax.dot_general(a, b, (((1,), (1,)), ((), ())), preferred_element_type=jnp.float32)


def lane_sum(weights):
    parts = [weights[:, i : i + HEAD] for i in range(0, weights.shape[1], HEAD)]
    while len(parts) > 1:
        parts = [a + b for a, b in zip(parts[::2], parts[1::2])]
    return parts[0]


def own_masks(own_ref):
    ids = own_ref[2 * BLOCK :, :].astype(jnp.float32)
    key_ids = jnp.concatenate([ids[0:1, :], ids[1:2, :]], axis=1)
    key_ids = jnp.broadcast_to(key_ids, (BLOCK, BLOCK))
    query_ids = key_ids.T
    q_pos = lax.broadcasted_iota(jnp.int32, (BLOCK, BLOCK), 0)
    k_pos = lax.broadcasted_iota(jnp.int32, (BLOCK, BLOCK), 1)
    visible = (key_ids == query_ids) & (k_pos <= q_pos)
    in_first = (query_ids == key_ids[0:1, 0:1])[:, :HEAD]
    return visible, in_first


def own_kernel(q_ref, own_ref, l_ref, acc_ref, first_ref):
    visible, in_first = own_masks(own_ref)
    first_ref[...] = jnp.where(in_first, 1.0, 0.0)
    keys = own_ref[:BLOCK, :]
    values = own_ref[BLOCK : 2 * BLOCK, :]
    for h in range(HEADS):
        rows = pl.ds(h * BLOCK, BLOCK)
        scores = contract_last(q_ref[:, h * HEAD : (h + 1) * HEAD], keys) * FACTOR
        weights = jnp.exp2(jnp.where(visible, scores, NEGATIVE))
        l_ref[rows, :] = lane_sum(weights)
        acc_ref[rows, :] = jnp.dot(
            weights.astype(jnp.bfloat16), values, preferred_element_type=jnp.float32
        )


def seen_rows(first_id, ids):
    ids = ids.astype(jnp.float32)
    return jnp.sum(jnp.where(ids == first_id, 1.0, 0.0)).astype(jnp.int32)


def add_blocks(slots, counts, ok_ref, q_ref, own_ref, l_sum, acc_sum, k_buf, v_buf, part):
    first_id = own_ref[2 * BLOCK :, :].astype(jnp.float32)[0:1, 0:1]
    full = jnp.int32(0)
    partial = jnp.int32(0)
    at = 0
    for ref, count in zip(slots, counts):
        for k in range(count):
            base = k * SLOT
            seen = seen_rows(first_id, ref[base + 2 * BLOCK : base + SLOT, :]) * ok_ref[at]
            at += 1
            whole = seen == BLOCK

            @pl.when(whole)
            def _():
                to = pl.ds(pl.multiple_of(full * BLOCK, BLOCK), BLOCK)
                k_buf[to, :] = ref[base : base + BLOCK, :]
                v_buf[to, :] = ref[base + BLOCK : base + 2 * BLOCK, :]

            @pl.when((seen > 0) & (seen < BLOCK))
            def _():
                part[...] = ref[base : base + 2 * BLOCK, :]

            full = full + whole.astype(jnp.int32)
            partial = partial + jnp.where(whole, 0, seen)

    def attend(chunk, limit):
        at = pl.ds(pl.multiple_of(chunk * WIDE, WIDE), WIDE)
        keys, values = k_buf[at, :], v_buf[at, :]
        for h in range(0, HEADS, TOGETHER):
            rows = pl.ds(h * BLOCK, TOGETHER * BLOCK)
            some = [q_ref[:, i * HEAD : (i + 1) * HEAD] for i in range(h, h + TOGETHER)]
            scores = contract_last(jnp.concatenate(some, axis=0), keys) * FACTOR
            if limit is not None:
                scores = scores + limit
            weights = jnp.exp2(scores)
            l_sum[rows, :] += lane_sum(weights)
            acc_sum[rows, :] += jnp.dot(
                weights.astype(jnp.bfloat16), values, preferred_element_type=jnp.float32
            )

    found = (full > 0) | (partial > 0)
    pairs = full // 2
    odd = full - 2 * pairs

    @pl.when(found)
    def _():
        l_sum[...] = jnp.zeros_like(l_sum)
        acc_sum[...] = jnp.zeros_like(acc_sum)

    @pl.loop(0, pairs)
    def _(chunk):
        attend(chunk, None)

    @pl.when((odd > 0) | (partial > 0))
    def _():
        left = pl.ds(pl.multiple_of(pairs * WIDE, WIDE), BLOCK)
        right = pl.ds(pl.multiple_of(pairs * WIDE + BLOCK, BLOCK), BLOCK)
        none = jnp.zeros((BLOCK, HEAD), jnp.bfloat16)

        @pl.when(odd == 0)
        def _():
            k_buf[left, :] = none
            v_buf[left, :] = none

        @pl.when(partial > 0)
        def _():
            k_buf[right, :] = part[:BLOCK, :]
            v_buf[right, :] = part[BLOCK:, :]

        @pl.when(partial == 0)
        def _():
            k_buf[right, :] = none
            v_buf[right, :] = none

        k_pos = lax.broadcasted_iota(jnp.int32, (1, WIDE), 1)
        shown = ((k_pos < BLOCK) & (odd > 0)) | (k_pos >= WIDE - partial)
        attend(pairs, jnp.where(shown, 0.0, NEGATIVE))

    return found


def more_kernel(counts, *refs):
    n = len(counts)
    ok_ref, q_ref, own_ref, l_in, acc_in, first_ref = refs[:6]
    slots = refs[6 : 6 + n]
    l_ref, acc_ref, l_sum, acc_sum, k_buf, v_buf, part = refs[6 + n :]
    found = add_blocks(
        slots, counts, ok_ref, q_ref, own_ref, l_sum, acc_sum, k_buf, v_buf, part
    )

    @pl.when(found)
    def _():
        keep = first_ref[...] > 0.0
        for h in range(HEADS):
            rows = pl.ds(h * BLOCK, BLOCK)
            l_ref[rows, :] = l_in[rows, :] + jnp.where(keep, l_sum[rows, :], 0.0)
            acc_ref[rows, :] = acc_in[rows, :] + jnp.where(keep, acc_sum[rows, :], 0.0)

    @pl.when(jnp.logical_not(found))
    def _():
        l_ref[...] = l_in[...]
        acc_ref[...] = acc_in[...]


def last_kernel(counts, all_counts, *refs):
    n, m = len(counts), len(all_counts)
    ok_ref, all_ok_ref, q_ref, own_ref, l_in, acc_in, first_ref = refs[:7]
    slots, everything = refs[7 : 7 + n], refs[7 + n : 7 + n + m]
    out_ref, l_sum, acc_sum, k_buf, v_buf, part, store, top, sem = refs[7 + n + m :]
    found = add_blocks(
        slots, counts, ok_ref, q_ref, own_ref, l_sum, acc_sum, k_buf, v_buf, part
    )

    @pl.when(jnp.logical_not(found))
    def _():
        l_sum[...] = jnp.zeros_like(l_sum)
        acc_sum[...] = jnp.zeros_like(acc_sum)

    keep = first_ref[...] > 0.0
    fine = jnp.ones((BLOCK, 1), jnp.float32)
    for h in range(HEADS):
        rows = pl.ds(h * BLOCK, BLOCK)
        total = l_in[rows, :] + jnp.where(keep, l_sum[rows, :], 0.0)
        total = jnp.sum(total, axis=1, keepdims=True)
        fine = jnp.where((total >= LOW) & (total <= HIGH), fine, 0.0)
        weighted = acc_in[rows, :] + jnp.where(keep, acc_sum[rows, :], 0.0)
        out_ref[:, h * HEAD : (h + 1) * HEAD] = (weighted / total).astype(jnp.bfloat16)

    @pl.when(jnp.min(fine) < 0.5)
    def _():
        at = 0
        for ref, count in zip(everything, all_counts):
            for k in range(count):
                copy = pltpu.make_async_copy(
                    ref.at[k * SLOT : (k + 1) * SLOT, :], store.at[at], sem
                )
                copy.start()
                copy.wait()
                at += 1
        with_maximum(at, all_ok_ref, q_ref, own_ref, store, top, l_sum, acc_sum, out_ref)


def with_maximum(count, ok_ref, q_ref, own_ref, store, top, l_sum, acc_sum, out_ref):
    visible, in_first = own_masks(own_ref)
    first_id = own_ref[2 * BLOCK :, :].astype(jnp.float32)[0:1, 0:1]
    own_bias = jnp.where(visible, 0.0, NEGATIVE)

    def head(h, carry):
        q = q_ref[:, pl.ds(pl.multiple_of(h * HEAD, HEAD), HEAD)]
        scores = contract_last(q, own_ref[:BLOCK, :]) * FACTOR + own_bias
        first_top = jnp.max(scores, axis=1, keepdims=True)
        weights = jnp.exp2(scores - first_top)
        top[...] = jnp.where(in_first, jnp.broadcast_to(first_top, (BLOCK, HEAD)), -NEGATIVE)
        l_sum[:BLOCK, :] = lane_sum(weights)
        acc_sum[:BLOCK, :] = jnp.dot(
            weights.astype(jnp.bfloat16),
            own_ref[BLOCK : 2 * BLOCK, :],
            preferred_element_type=jnp.float32,
        )

        def block(j, carry):
            seen = seen_rows(first_id, store[j, 2 * BLOCK :, :]) * ok_ref[j]

            @pl.when(seen > 0)
            def _():
                k_pos = lax.broadcasted_iota(jnp.int32, (1, BLOCK), 1)
                limit = jnp.where(k_pos >= BLOCK - seen, 0.0, NEGATIVE)
                scores = contract_last(q, store[j, :BLOCK, :]) * FACTOR + limit
                old = top[...]
                new = jnp.maximum(old, jnp.max(scores, axis=1, keepdims=True))
                fade = jnp.exp2(old - new)
                weights = jnp.exp2(scores - new[:, 0:1])
                l_sum[:BLOCK, :] = l_sum[:BLOCK, :] * fade + lane_sum(weights)
                acc_sum[:BLOCK, :] = acc_sum[:BLOCK, :] * fade + jnp.dot(
                    weights.astype(jnp.bfloat16),
                    store[j, BLOCK : 2 * BLOCK, :],
                    preferred_element_type=jnp.float32,
                )
                top[...] = new

            return carry

        lax.fori_loop(0, count, block, 0)
        total = jnp.sum(l_sum[:BLOCK, :], axis=1, keepdims=True)
        out_ref[:, pl.ds(pl.multiple_of(h * HEAD, HEAD), HEAD)] = (
            acc_sum[:BLOCK, :] / total
        ).astype(jnp.bfloat16)
        return carry

    lax.fori_loop(0, HEADS, head, 0)


VMEM = pl.BlockSpec(memory_space=pltpu.VMEM)
SMEM = pl.BlockSpec(memory_space=pltpu.SMEM)
SUMS = jax.ShapeDtypeStruct((HEADS * BLOCK, HEAD), jnp.float32)
FIRST = jax.ShapeDtypeStruct((BLOCK, HEAD), jnp.float32)
PARAMS = pltpu.CompilerParams(vmem_limit_bytes=24 * 1024 * 1024)


def cost(blocks):
    pairs = blocks
    return pl.CostEstimate(
        flops=4 * HEAD * pairs, bytes_accessed=1, transcendentals=pairs
    )


def buffers(blocks):
    rows = (blocks + blocks % 2 + 2) * BLOCK
    return [
        pltpu.VMEM(SUMS.shape, jnp.float32),
        pltpu.VMEM(SUMS.shape, jnp.float32),
        pltpu.VMEM((rows, HEAD), jnp.bfloat16),
        pltpu.VMEM((rows, HEAD), jnp.bfloat16),
        pltpu.VMEM((2 * BLOCK, HEAD), jnp.bfloat16),
    ]


def attend_own(q, own):
    return pl.pallas_call(
        own_kernel, out_shape=[SUMS, SUMS, FIRST], in_specs=[VMEM] * 2, out_specs=[VMEM] * 3,
        compiler_params=PARAMS, cost_estimate=cost(1), name="attend_own",
    )(q, own)


def stack_ok(ok):
    return jnp.stack([jnp.asarray(o, jnp.int32) for o in ok])


def attend_more(state, q, own, arrays, ok):
    counts = [a.shape[0] // SLOT for a in arrays]
    sums = pl.pallas_call(
        functools.partial(more_kernel, counts),
        out_shape=[SUMS, SUMS],
        in_specs=[SMEM] + [VMEM] * (5 + len(arrays)),
        out_specs=[VMEM] * 2,
        scratch_shapes=buffers(sum(counts)),
        compiler_params=PARAMS, cost_estimate=cost(sum(counts)), name="attend_more",
    )(stack_ok(ok), q, own, *state, *arrays)
    return *sums, state[2]


def attend_last(state, q, own, arrays, ok, everything, all_ok):
    counts = [a.shape[0] // SLOT for a in arrays]
    all_counts = [a.shape[0] // SLOT for a in everything]
    return pl.pallas_call(
        functools.partial(last_kernel, counts, all_counts),
        out_shape=jax.ShapeDtypeStruct((BLOCK, HEADS * HEAD), jnp.bfloat16),
        in_specs=[SMEM] * 2 + [VMEM] * (5 + len(arrays))
        + [pl.BlockSpec(memory_space=pl.ANY)] * len(everything),
        out_specs=VMEM,
        scratch_shapes=buffers(sum(counts))
        + [
            pltpu.VMEM((sum(all_counts), SLOT, HEAD), jnp.bfloat16),
            pltpu.VMEM((BLOCK, HEAD), jnp.float32),
            pltpu.SemaphoreType.DMA,
        ],
        compiler_params=PARAMS, cost_estimate=cost(sum(counts)), name="attend_last",
    )(stack_ok(ok), stack_ok(all_ok), q, own, *state, *arrays, *everything)


def exchange(v, mask):
    return lax.ppermute(v, "ctx", [(i, i ^ mask) for i in range(NX * NZ)])


def along_x(v, steps):
    return lax.ppermute(v, "ctx", [(i, i + NZ * steps) for i in range((NX - steps) * NZ)])


def together(*arrays):
    return lax.optimization_barrier(arrays)


def per_device(queries, keys, values, doc_ids):
    z = lax.axis_index("ctx") % NZ
    bit = [(z >> b) & 1 for b in range(3)]
    one = jnp.int32(1)
    ids = (doc_ids + 1).astype(jnp.bfloat16).reshape(2, HEAD)
    ids = jnp.pad(ids, ((0, IDS - 2), (0, 0)))
    own = jnp.concatenate([keys, values, ids], axis=0)
    q = queries

    p1 = exchange(own, 4)
    state = attend_own(q, own)
    state, p1 = together(state, p1)

    pair = jnp.concatenate([own, p1])
    b01 = along_x(pair, 1)
    c01 = along_x(pair, 2)
    p2 = exchange(pair, 2)
    state = attend_more(state, q, own, [p1], [bit[2]])
    state, p2, b01, c01 = together(state, p2, b01, c01)

    send = jnp.where(bit[0] == 0, own, c01[:SLOT])
    near0 = exchange(jnp.concatenate([b01[:SLOT], send]), 1)
    b2 = along_x(p2, 1)
    c2 = along_x(p2, 2)
    p3 = exchange(p2, 1)
    state = attend_more(state, q, own, [p2, b01, c01], [bit[1], bit[2]] + [one] * 4)
    state, near0, b2, c2, p3 = together(state, near0, b2, c2, p3)

    send = jnp.where(bit[2] == 1, p1, c01[SLOT:])
    near1 = exchange(jnp.concatenate([b01[SLOT:], send]), 1)
    b3 = along_x(p3, 1)
    c3 = exchange(c2, 1)
    state = attend_more(
        state, q, own, [near0, b2, c2, p3], [one] * 6 + [bit[1], bit[2]]
    )
    state, near1, b3, c3 = together(state, near1, b3, c3)

    arrays = [p1, p2, b01, c01, near0, b2, c2, p3, near1, b3, c3]
    ok = [bit[2], bit[1], bit[2]] + [one] * 10 + [bit[1], bit[2]] + [one] * 6
    return attend_last(state, q, own, [near1, b3, c3], [one] * 6, arrays, ok)


def solution(mesh):
    return jax.shard_map(
        per_device,
        mesh=mesh,
        in_specs=(
            P(("dp", "ctx"), "tp"),
            P(("dp", "ctx"), "tp"),
            P(("dp", "ctx"), "tp"),
            P(("dp", "ctx")),
        ),
        out_specs=P(("dp", "ctx"), "tp"),
        check_vma=False,
    )
```

```python
import functools
import math

import jax
import jax.numpy as jnp
from jax import lax
from jax.experimental import pallas as pl
from jax.experimental.pallas import tpu as pltpu
from jax.sharding import PartitionSpec as P

HEAD = 128
BLOCK = 256
HEADS = 8
TOGETHER = 4
IDS = 16
SLOT = 2 * BLOCK + IDS
WIDE = 2 * BLOCK
NX, NZ = 4, 8
NEGATIVE = -1e30
FACTOR = HEAD**-0.5 * math.log2(math.e)
HIGH = 2.0**100


def contract_last(a, b):
    return lax.dot_general(a, b, (((1,), (1,)), ((), ())), preferred_element_type=jnp.float32)


def lane_sum(weights):
    parts = [weights[:, i : i + HEAD] for i in range(0, weights.shape[1], HEAD)]
    while len(parts) > 1:
        parts = [a + b for a, b in zip(parts[::2], parts[1::2])]
    return parts[0]


def own_masks(own_ref):
    ids = own_ref[2 * BLOCK :, :].astype(jnp.float32)
    key_ids = jnp.concatenate([ids[0:1, :], ids[1:2, :]], axis=1)
    key_ids = jnp.broadcast_to(key_ids, (BLOCK, BLOCK))
    query_ids = key_ids.T
    q_pos = lax.broadcasted_iota(jnp.int32, (BLOCK, BLOCK), 0)
    k_pos = lax.broadcasted_iota(jnp.int32, (BLOCK, BLOCK), 1)
    visible = (key_ids == query_ids) & (k_pos <= q_pos)
    in_first = (query_ids == key_ids[0:1, 0:1])[:, :HEAD]
    return visible, in_first


def own_kernel(q_ref, own_ref, shift_ref, l_ref, acc_ref):
    visible, in_first = own_masks(own_ref)
    keys = own_ref[:BLOCK, :]
    values = own_ref[BLOCK : 2 * BLOCK, :]
    for h in range(HEADS):
        rows = pl.ds(h * BLOCK, BLOCK)
        scores = contract_last(q_ref[:, h * HEAD : (h + 1) * HEAD], keys) * FACTOR
        scores = jnp.where(visible, scores, NEGATIVE)
        top = jnp.max(scores, axis=1, keepdims=True)
        weights = jnp.exp2(scores - top)
        l_ref[rows, :] = lane_sum(weights)
        acc_ref[rows, :] = jnp.dot(
            weights.astype(jnp.bfloat16), values, preferred_element_type=jnp.float32
        )
        shift_ref[rows, :] = jnp.where(
            in_first, jnp.broadcast_to(top, (BLOCK, HEAD)), -NEGATIVE
        )


def seen_rows(first_id, ids):
    ids = ids.astype(jnp.float32)
    return jnp.sum(jnp.where(ids == first_id, 1.0, 0.0)).astype(jnp.int32)


def add_blocks(slots, counts, ok_ref, q_ref, own_ref, shift_ref, l_ref, acc_ref, k_buf, v_buf, part):
    first_id = own_ref[2 * BLOCK :, :].astype(jnp.float32)[0:1, 0:1]
    full = jnp.int32(0)
    partial = jnp.int32(0)
    at = 0
    for ref, count in zip(slots, counts):
        for k in range(count):
            base = k * SLOT
            seen = seen_rows(first_id, ref[base + 2 * BLOCK : base + SLOT, :]) * ok_ref[at]
            at += 1
            whole = seen == BLOCK

            @pl.when(whole)
            def _():
                to = pl.ds(pl.multiple_of(full * BLOCK, BLOCK), BLOCK)
                k_buf[to, :] = ref[base : base + BLOCK, :]
                v_buf[to, :] = ref[base + BLOCK : base + 2 * BLOCK, :]

            @pl.when((seen > 0) & (seen < BLOCK))
            def _():
                part[...] = ref[base : base + 2 * BLOCK, :]

            full = full + whole.astype(jnp.int32)
            partial = partial + jnp.where(whole, 0, seen)

    def attend(chunk, limit):
        at = pl.ds(pl.multiple_of(chunk * WIDE, WIDE), WIDE)
        keys, values = k_buf[at, :], v_buf[at, :]
        for h in range(0, HEADS, TOGETHER):
            rows = pl.ds(h * BLOCK, TOGETHER * BLOCK)
            some = [q_ref[:, i * HEAD : (i + 1) * HEAD] for i in range(h, h + TOGETHER)]
            scores = contract_last(jnp.concatenate(some, axis=0), keys) * FACTOR
            if limit is not None:
                scores = scores + limit
            shift = shift_ref[rows, :]
            weights = jnp.exp2(scores - jnp.concatenate([shift] * (WIDE // HEAD), axis=1))
            l_ref[rows, :] += lane_sum(weights)
            acc_ref[rows, :] += jnp.dot(
                weights.astype(jnp.bfloat16), values, preferred_element_type=jnp.float32
            )

    pairs = full // 2
    odd = full - 2 * pairs

    @pl.loop(0, pairs)
    def _(chunk):
        attend(chunk, None)

    @pl.when((odd > 0) | (partial > 0))
    def _():
        left = pl.ds(pl.multiple_of(pairs * WIDE, WIDE), BLOCK)
        right = pl.ds(pl.multiple_of(pairs * WIDE + BLOCK, BLOCK), BLOCK)
        none = jnp.zeros((BLOCK, HEAD), jnp.bfloat16)

        @pl.when(odd == 0)
        def _():
            k_buf[left, :] = none
            v_buf[left, :] = none

        @pl.when(partial > 0)
        def _():
            k_buf[right, :] = part[:BLOCK, :]
            v_buf[right, :] = part[BLOCK:, :]

        @pl.when(partial == 0)
        def _():
            k_buf[right, :] = none
            v_buf[right, :] = none

        k_pos = lax.broadcasted_iota(jnp.int32, (1, WIDE), 1)
        shown = ((k_pos < BLOCK) & (odd > 0)) | (k_pos >= WIDE - partial)
        attend(pairs, jnp.where(shown, 0.0, NEGATIVE))


def more_kernel(counts, *refs):
    n = len(counts)
    ok_ref, q_ref, own_ref, shift_ref, l_in, acc_in = refs[:6]
    slots = refs[6 : 6 + n]
    l_ref, acc_ref, k_buf, v_buf, part = refs[6 + n :]
    l_ref[...] = l_in[...]
    acc_ref[...] = acc_in[...]
    add_blocks(
        slots, counts, ok_ref, q_ref, own_ref, shift_ref, l_ref, acc_ref, k_buf, v_buf, part
    )


def last_kernel(counts, all_counts, *refs):
    n, m = len(counts), len(all_counts)
    ok_ref, all_ok_ref, q_ref, own_ref, shift_ref, l_in, acc_in = refs[:7]
    slots, everything = refs[7 : 7 + n], refs[7 + n : 7 + n + m]
    out_ref, l_ref, acc_ref, k_buf, v_buf, part, store, top, sem = refs[7 + n + m :]
    l_ref[...] = l_in[...]
    acc_ref[...] = acc_in[...]
    add_blocks(
        slots, counts, ok_ref, q_ref, own_ref, shift_ref, l_ref, acc_ref, k_buf, v_buf, part
    )
    most = jnp.zeros((BLOCK, 1), jnp.float32)
    for h in range(HEADS):
        rows = pl.ds(h * BLOCK, BLOCK)
        total = jnp.sum(l_ref[rows, :], axis=1, keepdims=True)
        most = jnp.where(total <= HIGH, most, 1.0)
        out_ref[:, h * HEAD : (h + 1) * HEAD] = (acc_ref[rows, :] * (1.0 / total)).astype(
            jnp.bfloat16
        )

    @pl.when(jnp.max(most) > 0.5)
    def _():
        at = 0
        for ref, count in zip(everything, all_counts):
            for k in range(count):
                copy = pltpu.make_async_copy(
                    ref.at[k * SLOT : (k + 1) * SLOT, :], store.at[at], sem
                )
                copy.start()
                copy.wait()
                at += 1
        with_maximum(at, all_ok_ref, q_ref, own_ref, store, top, l_ref, acc_ref, out_ref)


def with_maximum(count, ok_ref, q_ref, own_ref, store, top, l_sum, acc_sum, out_ref):
    visible, in_first = own_masks(own_ref)
    first_id = own_ref[2 * BLOCK :, :].astype(jnp.float32)[0:1, 0:1]
    own_bias = jnp.where(visible, 0.0, NEGATIVE)

    def head(h, carry):
        q = q_ref[:, pl.ds(pl.multiple_of(h * HEAD, HEAD), HEAD)]
        scores = contract_last(q, own_ref[:BLOCK, :]) * FACTOR + own_bias
        first_top = jnp.max(scores, axis=1, keepdims=True)
        weights = jnp.exp2(scores - first_top)
        top[...] = jnp.where(in_first, jnp.broadcast_to(first_top, (BLOCK, HEAD)), -NEGATIVE)
        l_sum[:BLOCK, :] = lane_sum(weights)
        acc_sum[:BLOCK, :] = jnp.dot(
            weights.astype(jnp.bfloat16),
            own_ref[BLOCK : 2 * BLOCK, :],
            preferred_element_type=jnp.float32,
        )

        def block(j, carry):
            seen = seen_rows(first_id, store[j, 2 * BLOCK :, :]) * ok_ref[j]

            @pl.when(seen > 0)
            def _():
                k_pos = lax.broadcasted_iota(jnp.int32, (1, BLOCK), 1)
                limit = jnp.where(k_pos >= BLOCK - seen, 0.0, NEGATIVE)
                scores = contract_last(q, store[j, :BLOCK, :]) * FACTOR + limit
                old = top[...]
                new = jnp.maximum(old, jnp.max(scores, axis=1, keepdims=True))
                fade = jnp.exp2(old - new)
                weights = jnp.exp2(scores - new[:, 0:1])
                l_sum[:BLOCK, :] = l_sum[:BLOCK, :] * fade + lane_sum(weights)
                acc_sum[:BLOCK, :] = acc_sum[:BLOCK, :] * fade + jnp.dot(
                    weights.astype(jnp.bfloat16),
                    store[j, BLOCK : 2 * BLOCK, :],
                    preferred_element_type=jnp.float32,
                )
                top[...] = new

            return carry

        lax.fori_loop(0, count, block, 0)
        total = jnp.sum(l_sum[:BLOCK, :], axis=1, keepdims=True)
        out_ref[:, pl.ds(pl.multiple_of(h * HEAD, HEAD), HEAD)] = (
            acc_sum[:BLOCK, :] * (1.0 / total)
        ).astype(jnp.bfloat16)
        return carry

    lax.fori_loop(0, HEADS, head, 0)


VMEM = pl.BlockSpec(memory_space=pltpu.VMEM)
SMEM = pl.BlockSpec(memory_space=pltpu.SMEM)
SUMS = jax.ShapeDtypeStruct((HEADS * BLOCK, HEAD), jnp.float32)
COST = pl.CostEstimate(flops=1, bytes_accessed=1, transcendentals=0)


def params(mib):
    return pltpu.CompilerParams(vmem_limit_bytes=mib * 1024 * 1024)


def buffers(blocks):
    rows = (blocks + blocks % 2 + 2) * BLOCK
    return [
        pltpu.VMEM((rows, HEAD), jnp.bfloat16),
        pltpu.VMEM((rows, HEAD), jnp.bfloat16),
        pltpu.VMEM((2 * BLOCK, HEAD), jnp.bfloat16),
    ]


def attend_own(q, own):
    return pl.pallas_call(
        own_kernel, out_shape=[SUMS] * 3, in_specs=[VMEM] * 2, out_specs=[VMEM] * 3,
        compiler_params=params(12), cost_estimate=COST, name="attend_own",
    )(q, own)


def stack_ok(ok):
    return jnp.stack([jnp.asarray(o, jnp.int32) for o in ok])


def attend_more(state, q, own, arrays, ok):
    counts = [a.shape[0] // SLOT for a in arrays]
    sums = pl.pallas_call(
        functools.partial(more_kernel, counts),
        out_shape=[SUMS] * 2,
        in_specs=[SMEM] + [VMEM] * (5 + len(arrays)),
        out_specs=[VMEM] * 2,
        scratch_shapes=buffers(sum(counts)),
        compiler_params=params(12), cost_estimate=COST, name="attend_more",
    )(stack_ok(ok), q, own, *state, *arrays)
    return state[0], *sums


def attend_last(state, q, own, arrays, ok, everything, all_ok):
    counts = [a.shape[0] // SLOT for a in arrays]
    all_counts = [a.shape[0] // SLOT for a in everything]
    return pl.pallas_call(
        functools.partial(last_kernel, counts, all_counts),
        out_shape=jax.ShapeDtypeStruct((BLOCK, HEADS * HEAD), jnp.bfloat16),
        in_specs=[SMEM] * 2 + [VMEM] * (5 + len(arrays))
        + [pl.BlockSpec(memory_space=pl.ANY)] * len(everything),
        out_specs=VMEM,
        scratch_shapes=[pltpu.VMEM(SUMS.shape, jnp.float32)] * 2
        + buffers(sum(counts))
        + [
            pltpu.VMEM((sum(all_counts), SLOT, HEAD), jnp.bfloat16),
            pltpu.VMEM((BLOCK, HEAD), jnp.float32),
            pltpu.SemaphoreType.DMA,
        ],
        compiler_params=params(16), cost_estimate=COST, name="attend_last",
    )(stack_ok(ok), stack_ok(all_ok), q, own, *state, *arrays, *everything)


def exchange(v, mask):
    return lax.ppermute(v, "ctx", [(i, i ^ mask) for i in range(NX * NZ)])


def along_x(v, steps):
    return lax.ppermute(v, "ctx", [(i, i + NZ * steps) for i in range((NX - steps) * NZ)])


def together(*arrays):
    return lax.optimization_barrier(arrays)


def per_device(queries, keys, values, doc_ids):
    z = lax.axis_index("ctx") % NZ
    bit = [(z >> b) & 1 for b in range(3)]
    one = jnp.int32(1)
    ids = (doc_ids + 1).astype(jnp.bfloat16).reshape(2, HEAD)
    ids = jnp.pad(ids, ((0, IDS - 2), (0, 0)))
    own = jnp.concatenate([keys, values, ids], axis=0)
    q = queries

    p4 = exchange(own, 4)
    p2 = exchange(own, 2)
    state = attend_own(q, own)
    state, out = together(state, own)
    b0 = along_x(out, 1)
    c0 = along_x(out, 2)
    state, p2, p4, b0, c0 = together(state, p2, p4, b0, c0)

    near1 = exchange(jnp.concatenate([b0, jnp.where(bit[0] == 0, own, c0)]), 1)
    pair = jnp.concatenate([p2, p4])
    b24 = along_x(pair, 1)
    c24 = along_x(pair, 2)
    p6 = exchange(p4, 2)
    state = attend_more(state, q, own, [p2, p4, b0, c0], [bit[1], bit[2], one, one])
    state, p6, b24, c24 = together(state, p6, b24, c24)

    sent = [
        b24,
        jnp.where(bit[1] == 1, p2, c24[:SLOT]),
        jnp.where(bit[2] == 1, p4, c24[SLOT:]),
    ]
    near35 = exchange(jnp.concatenate(sent), 1)
    b6 = along_x(p6, 1)
    c6 = along_x(p6, 2)
    state = attend_more(state, q, own, [near1, b24, c24, p6], [one] * 6 + [bit[2]])
    state, b6, c6 = together(state, b6, c6)

    near7 = exchange(jnp.concatenate([b6, jnp.where(bit[2] == 1, p6, c6)]), 1)
    state = attend_more(state, q, own, [near35, b6, c6], [one] * 6)
    arrays = [p2, p4, b0, c0, near1, b24, c24, p6, near35, b6, c6, near7]
    ok = [bit[1], bit[2]] + [one] * 8 + [bit[2]] + [one] * 8
    return attend_last(state, q, own, [near7], [one] * 2, arrays, ok)


def solution(mesh):
    return jax.shard_map(
        per_device,
        mesh=mesh,
        in_specs=(
            P(("dp", "ctx"), "tp"),
            P(("dp", "ctx"), "tp"),
            P(("dp", "ctx"), "tp"),
            P(("dp", "ctx")),
        ),
        out_specs=P(("dp", "ctx"), "tp"),
        check_vma=False,
    )
```

```python
import functools
import math

import jax
import jax.numpy as jnp
from jax import lax
from jax.experimental import pallas as pl
from jax.experimental.pallas import tpu as pltpu
from jax.sharding import PartitionSpec as P

HEAD = 128
BLOCK = 256
HEADS = 8
TOGETHER = 4
IDS = 16
SLOT = 2 * BLOCK + IDS
WIDE = 2 * BLOCK
NX, NZ = 4, 8
NEGATIVE = -1e30
FACTOR = HEAD**-0.5 * math.log2(math.e)
HIGH = 2.0**100
VMEM_MIB = 16


def contract_last(a, b):
    return lax.dot_general(a, b, (((1,), (1,)), ((), ())), preferred_element_type=jnp.float32)


def lane_sum(weights):
    parts = [weights[:, i : i + HEAD] for i in range(0, weights.shape[1], HEAD)]
    while len(parts) > 1:
        parts = [a + b for a, b in zip(parts[::2], parts[1::2])]
    return parts[0]


def own_masks(own_ref):
    ids = own_ref[2 * BLOCK :, :].astype(jnp.float32)
    key_ids = jnp.concatenate([ids[0:1, :], ids[1:2, :]], axis=1)
    key_ids = jnp.broadcast_to(key_ids, (BLOCK, BLOCK))
    query_ids = key_ids.T
    q_pos = lax.broadcasted_iota(jnp.int32, (BLOCK, BLOCK), 0)
    k_pos = lax.broadcasted_iota(jnp.int32, (BLOCK, BLOCK), 1)
    visible = (key_ids == query_ids) & (k_pos <= q_pos)
    in_first = (query_ids == key_ids[0:1, 0:1])[:, :HEAD]
    return visible, in_first


def add_own(q_ref, own_ref, shift_ref, l_ref, acc_ref):
    visible, in_first = own_masks(own_ref)
    keys = own_ref[:BLOCK, :]
    values = own_ref[BLOCK : 2 * BLOCK, :]
    for h in range(HEADS):
        rows = pl.ds(h * BLOCK, BLOCK)
        scores = contract_last(q_ref[:, h * HEAD : (h + 1) * HEAD], keys) * FACTOR
        scores = jnp.where(visible, scores, NEGATIVE)
        top = jnp.max(scores, axis=1, keepdims=True)
        weights = jnp.exp2(scores - top)
        l_ref[rows, :] = lane_sum(weights)
        acc_ref[rows, :] = jnp.dot(
            weights.astype(jnp.bfloat16), values, preferred_element_type=jnp.float32
        )
        shift_ref[rows, :] = jnp.where(
            in_first, jnp.broadcast_to(top, (BLOCK, HEAD)), -NEGATIVE
        )


def seen_rows(first_id, ids):
    ids = ids.astype(jnp.float32)
    return jnp.sum(jnp.where(ids == first_id, 1.0, 0.0)).astype(jnp.int32)


def gather(slots, counts, ok_ref, own_ref, k_buf, v_buf, part):
    first_id = own_ref[2 * BLOCK :, :].astype(jnp.float32)[0:1, 0:1]
    full = jnp.int32(0)
    partial = jnp.int32(0)
    at = 0
    for ref, count in zip(slots, counts):
        for k in range(count):
            base = k * SLOT
            seen = seen_rows(first_id, ref[base + 2 * BLOCK : base + SLOT, :]) * ok_ref[at]
            at += 1
            whole = seen == BLOCK

            @pl.when(whole)
            def _():
                to = pl.ds(pl.multiple_of(full * BLOCK, BLOCK), BLOCK)
                k_buf[to, :] = ref[base : base + BLOCK, :]
                v_buf[to, :] = ref[base + BLOCK : base + 2 * BLOCK, :]

            @pl.when((seen > 0) & (seen < BLOCK))
            def _():
                part[...] = ref[base : base + 2 * BLOCK, :]

            full = full + whole.astype(jnp.int32)
            partial = partial + jnp.where(whole, 0, seen)
    return full, partial


def add_blocks(full, partial, q_ref, shift_ref, l_ref, acc_ref, k_buf, v_buf, part):
    def attend(chunk, limit):
        at = pl.ds(pl.multiple_of(chunk * WIDE, WIDE), WIDE)
        keys, values = k_buf[at, :], v_buf[at, :]
        for h in range(0, HEADS, TOGETHER):
            rows = pl.ds(h * BLOCK, TOGETHER * BLOCK)
            some = [q_ref[:, i * HEAD : (i + 1) * HEAD] for i in range(h, h + TOGETHER)]
            scores = contract_last(jnp.concatenate(some, axis=0), keys) * FACTOR
            if limit is not None:
                scores = scores + limit
            shift = shift_ref[rows, :]
            weights = jnp.exp2(scores - jnp.concatenate([shift] * (WIDE // HEAD), axis=1))
            l_ref[rows, :] += lane_sum(weights)
            acc_ref[rows, :] += jnp.dot(
                weights.astype(jnp.bfloat16), values, preferred_element_type=jnp.float32
            )

    pairs = full // 2
    odd = full - 2 * pairs

    @pl.loop(0, pairs)
    def _(chunk):
        attend(chunk, None)

    @pl.when((odd > 0) | (partial > 0))
    def _():
        left = pl.ds(pl.multiple_of(pairs * WIDE, WIDE), BLOCK)
        right = pl.ds(pl.multiple_of(pairs * WIDE + BLOCK, BLOCK), BLOCK)
        none = jnp.zeros((BLOCK, HEAD), jnp.bfloat16)

        @pl.when(odd == 0)
        def _():
            k_buf[left, :] = none
            v_buf[left, :] = none

        @pl.when(partial > 0)
        def _():
            k_buf[right, :] = part[:BLOCK, :]
            v_buf[right, :] = part[BLOCK:, :]

        @pl.when(partial == 0)
        def _():
            k_buf[right, :] = none
            v_buf[right, :] = none

        k_pos = lax.broadcasted_iota(jnp.int32, (1, WIDE), 1)
        shown = ((k_pos < BLOCK) & (odd > 0)) | (k_pos >= WIDE - partial)
        attend(pairs, jnp.where(shown, 0.0, NEGATIVE))


def copies(pairs, sems):
    return [pltpu.make_async_copy(a, b, sems.at[i]) for i, (a, b) in enumerate(pairs)]


def run(moves):
    for move in moves:
        move.start()
    for move in moves:
        move.wait()


def first_kernel(counts, *refs):
    n = len(counts)
    ok_ref, q_hbm, own_ref = refs[:3]
    slots = refs[3 : 3 + n]
    shift_out, l_out, acc_out, q, shift, l_sum, acc_sum, k_buf, v_buf, part, sems = refs[3 + n :]
    fetch, *keep = copies(
        [(q_hbm, q), (shift, shift_out), (l_sum, l_out), (acc_sum, acc_out)], sems
    )
    fetch.start()
    full, partial = gather(slots, counts, ok_ref, own_ref, k_buf, v_buf, part)
    fetch.wait()
    add_own(q, own_ref, shift, l_sum, acc_sum)
    keep[0].start()
    add_blocks(full, partial, q, shift, l_sum, acc_sum, k_buf, v_buf, part)
    keep[1].start()
    keep[2].start()
    for move in keep:
        move.wait()


def more_kernel(counts, *refs):
    n = len(counts)
    ok_ref, q_hbm, own_ref, shift_in, l_in, acc_in = refs[:6]
    slots = refs[6 : 6 + n]
    l_out, acc_out, q, shift, l_sum, acc_sum, k_buf, v_buf, part, sems = refs[6 + n :]
    full, partial = gather(slots, counts, ok_ref, own_ref, k_buf, v_buf, part)

    @pl.when((full > 0) | (partial > 0))
    def _():
        run(copies([(q_hbm, q), (shift_in, shift), (l_in, l_sum), (acc_in, acc_sum)], sems))
        add_blocks(full, partial, q, shift, l_sum, acc_sum, k_buf, v_buf, part)
        run(copies([(l_sum, l_out), (acc_sum, acc_out)], sems))


def last_kernel(counts, all_counts, *refs):
    n, m = len(counts), len(all_counts)
    ok_ref, all_ok_ref, q_hbm, own_ref, shift_in, l_in, acc_in = refs[:7]
    slots, everything = refs[7 : 7 + n], refs[7 + n : 7 + n + m]
    out_ref, q, shift, l_sum, acc_sum, k_buf, v_buf, part, sems, store, top = refs[7 + n + m :]
    moves = copies([(q_hbm, q), (shift_in, shift), (l_in, l_sum), (acc_in, acc_sum)], sems)
    for move in moves:
        move.start()
    full, partial = gather(slots, counts, ok_ref, own_ref, k_buf, v_buf, part)
    for move in moves:
        move.wait()
    add_blocks(full, partial, q, shift, l_sum, acc_sum, k_buf, v_buf, part)
    most = jnp.zeros((BLOCK, 1), jnp.float32)
    for h in range(HEADS):
        rows = pl.ds(h * BLOCK, BLOCK)
        total = jnp.sum(l_sum[rows, :], axis=1, keepdims=True)
        most = jnp.where(total <= HIGH, most, 1.0)
        out_ref[:, h * HEAD : (h + 1) * HEAD] = (acc_sum[rows, :] * (1.0 / total)).astype(
            jnp.bfloat16
        )

    @pl.when(jnp.max(most) > 0.5)
    def _():
        at = 0
        for ref, count in zip(everything, all_counts):
            for k in range(count):
                run(copies([(ref.at[k * SLOT : (k + 1) * SLOT, :], store.at[at])], sems))
                at += 1
        with_maximum(at, all_ok_ref, q, own_ref, store, top, l_sum, acc_sum, out_ref)


def with_maximum(count, ok_ref, q_ref, own_ref, store, top, l_sum, acc_sum, out_ref):
    visible, in_first = own_masks(own_ref)
    first_id = own_ref[2 * BLOCK :, :].astype(jnp.float32)[0:1, 0:1]
    own_bias = jnp.where(visible, 0.0, NEGATIVE)

    def head(h, carry):
        q = q_ref[:, pl.ds(pl.multiple_of(h * HEAD, HEAD), HEAD)]
        scores = contract_last(q, own_ref[:BLOCK, :]) * FACTOR + own_bias
        first_top = jnp.max(scores, axis=1, keepdims=True)
        weights = jnp.exp2(scores - first_top)
        top[...] = jnp.where(in_first, jnp.broadcast_to(first_top, (BLOCK, HEAD)), -NEGATIVE)
        l_sum[:BLOCK, :] = lane_sum(weights)
        acc_sum[:BLOCK, :] = jnp.dot(
            weights.astype(jnp.bfloat16),
            own_ref[BLOCK : 2 * BLOCK, :],
            preferred_element_type=jnp.float32,
        )

        def block(j, carry):
            seen = seen_rows(first_id, store[j, 2 * BLOCK :, :]) * ok_ref[j]

            @pl.when(seen > 0)
            def _():
                k_pos = lax.broadcasted_iota(jnp.int32, (1, BLOCK), 1)
                limit = jnp.where(k_pos >= BLOCK - seen, 0.0, NEGATIVE)
                scores = contract_last(q, store[j, :BLOCK, :]) * FACTOR + limit
                old = top[...]
                new = jnp.maximum(old, jnp.max(scores, axis=1, keepdims=True))
                fade = jnp.exp2(old - new)
                weights = jnp.exp2(scores - new[:, 0:1])
                l_sum[:BLOCK, :] = l_sum[:BLOCK, :] * fade + lane_sum(weights)
                acc_sum[:BLOCK, :] = acc_sum[:BLOCK, :] * fade + jnp.dot(
                    weights.astype(jnp.bfloat16),
                    store[j, BLOCK : 2 * BLOCK, :],
                    preferred_element_type=jnp.float32,
                )
                top[...] = new

            return carry

        lax.fori_loop(0, count, block, 0)
        total = jnp.sum(l_sum[:BLOCK, :], axis=1, keepdims=True)
        out_ref[:, pl.ds(pl.multiple_of(h * HEAD, HEAD), HEAD)] = (
            acc_sum[:BLOCK, :] * (1.0 / total)
        ).astype(jnp.bfloat16)
        return carry

    lax.fori_loop(0, HEADS, head, 0)


VMEM = pl.BlockSpec(memory_space=pltpu.VMEM)
SMEM = pl.BlockSpec(memory_space=pltpu.SMEM)
HBM = pl.BlockSpec(memory_space=pltpu.HBM)
SUMS = jax.ShapeDtypeStruct((HEADS * BLOCK, HEAD), jnp.float32)
COST = pl.CostEstimate(flops=1, bytes_accessed=1, transcendentals=0)


def params(mib):
    return pltpu.CompilerParams(vmem_limit_bytes=mib * 1024 * 1024)


def buffers(blocks):
    rows = (blocks + blocks % 2 + 2) * BLOCK
    return [
        pltpu.VMEM((BLOCK, HEADS * HEAD), jnp.bfloat16),
        pltpu.VMEM(SUMS.shape, jnp.float32),
        pltpu.VMEM(SUMS.shape, jnp.float32),
        pltpu.VMEM(SUMS.shape, jnp.float32),
        pltpu.VMEM((rows, HEAD), jnp.bfloat16),
        pltpu.VMEM((rows, HEAD), jnp.bfloat16),
        pltpu.VMEM((2 * BLOCK, HEAD), jnp.bfloat16),
        pltpu.SemaphoreType.DMA((4,)),
    ]


def in_hbm(*arrays):
    return [pltpu.with_memory_space_constraint(a, pltpu.HBM) for a in arrays]


def stack_ok(ok):
    return jnp.stack([jnp.asarray(o, jnp.int32) for o in ok])


def attend_first(q, own, arrays, ok):
    counts = [a.shape[0] // SLOT for a in arrays]
    return pl.pallas_call(
        functools.partial(first_kernel, counts),
        out_shape=[pltpu.HBM(SUMS.shape, SUMS.dtype)] * 3,
        in_specs=[SMEM, HBM, VMEM] + [VMEM] * len(arrays),
        out_specs=[HBM] * 3,
        scratch_shapes=buffers(sum(counts)),
        compiler_params=params(VMEM_MIB), cost_estimate=COST, name="attend_first",
    )(stack_ok(ok), *in_hbm(q), own, *arrays)


def attend_more(state, q, own, arrays, ok):
    counts = [a.shape[0] // SLOT for a in arrays]
    sums = pl.pallas_call(
        functools.partial(more_kernel, counts),
        out_shape=[pltpu.HBM(SUMS.shape, SUMS.dtype)] * 2,
        in_specs=[SMEM, HBM, VMEM] + [HBM] * 3 + [VMEM] * len(arrays),
        out_specs=[HBM] * 2,
        scratch_shapes=buffers(sum(counts)),
        input_output_aliases={4: 0, 5: 1},
        compiler_params=params(VMEM_MIB), cost_estimate=COST, name="attend_more",
    )(stack_ok(ok), *in_hbm(q), own, *in_hbm(*state), *arrays)
    return state[0], *sums


def attend_last(state, q, own, arrays, ok, everything, all_ok):
    counts = [a.shape[0] // SLOT for a in arrays]
    all_counts = [a.shape[0] // SLOT for a in everything]
    return pl.pallas_call(
        functools.partial(last_kernel, counts, all_counts),
        out_shape=jax.ShapeDtypeStruct((BLOCK, HEADS * HEAD), jnp.bfloat16),
        in_specs=[SMEM] * 2 + [HBM, VMEM] + [HBM] * 3 + [VMEM] * len(arrays)
        + [pl.BlockSpec(memory_space=pl.ANY)] * len(everything),
        out_specs=VMEM,
        scratch_shapes=buffers(sum(counts))
        + [
            pltpu.VMEM((sum(all_counts), SLOT, HEAD), jnp.bfloat16),
            pltpu.VMEM((BLOCK, HEAD), jnp.float32),
        ],
        compiler_params=params(VMEM_MIB), cost_estimate=COST, name="attend_last",
    )(
        stack_ok(ok), stack_ok(all_ok), *in_hbm(q), own, *in_hbm(*state), *arrays, *everything
    )


def exchange(v, mask):
    return lax.ppermute(v, "ctx", [(i, i ^ mask) for i in range(NX * NZ)])


def along_x(v, steps):
    return lax.ppermute(v, "ctx", [(i, i + NZ * steps) for i in range((NX - steps) * NZ)])


def together(*arrays):
    return lax.optimization_barrier(arrays)


def per_device(queries, keys, values, doc_ids):
    z = lax.axis_index("ctx") % NZ
    bit = [(z >> b) & 1 for b in range(3)]
    one = jnp.int32(1)
    ids = (doc_ids + 1).astype(jnp.bfloat16).reshape(2, HEAD)
    ids = jnp.pad(ids, ((0, IDS - 2), (0, 0)))
    own = jnp.concatenate([keys, values, ids], axis=0)
    q = queries

    b0 = along_x(own, 1)
    c0 = along_x(own, 2)
    p2 = exchange(own, 2)
    p4 = exchange(own, 4)
    p4, p2, b0, c0 = together(p4, p2, b0, c0)

    near1 = exchange(jnp.concatenate([b0, jnp.where(bit[0] == 0, own, c0)]), 1)
    pair = jnp.concatenate([p2, p4])
    b24 = along_x(pair, 1)
    c24 = along_x(pair, 2)
    p6 = exchange(p4, 2)
    state = attend_first(q, own, [p4, p2, b0, c0], [bit[2], bit[1], one, one])
    state, p6, b24, c24 = together(state, p6, b24, c24)

    sent = [
        b24,
        jnp.where(bit[1] == 1, p2, c24[:SLOT]),
        jnp.where(bit[2] == 1, p4, c24[SLOT:]),
    ]
    near35 = exchange(jnp.concatenate(sent), 1)
    b6 = along_x(p6, 1)
    c6 = along_x(p6, 2)
    b6, c6 = together(b6, c6)

    near7 = exchange(jnp.concatenate([b6, jnp.where(bit[2] == 1, p6, c6)]), 1)
    state = attend_more(
        state, q, own, [near1, b24, c24, p6, b6, c6, near35], [one] * 6 + [bit[2]] + [one] * 6
    )
    arrays = [p2, p4, b0, c0, near1, b24, c24, p6, near35, b6, c6, near7]
    ok = [bit[1], bit[2]] + [one] * 8 + [bit[2]] + [one] * 8
    return attend_last(state, q, own, [near7], [one] * 2, arrays, ok)


def solution(mesh):
    return jax.shard_map(
        per_device,
        mesh=mesh,
        in_specs=(
            P(("dp", "ctx"), "tp"),
            P(("dp", "ctx"), "tp"),
            P(("dp", "ctx"), "tp"),
            P(("dp", "ctx")),
        ),
        out_specs=P(("dp", "ctx"), "tp"),
        check_vma=False,
    )
```

```python
import functools
import math

import jax
import jax.numpy as jnp
from jax import lax
from jax.experimental import pallas as pl
from jax.experimental.pallas import tpu as pltpu
from jax.sharding import PartitionSpec as P

HEAD = 128
BLOCK = 256
HEADS = 8
TOGETHER = 4
IDS = 16
SLOT = 2 * BLOCK + IDS
WIDE = 2 * BLOCK
NX, NZ = 4, 8
NEGATIVE = -1e30
FACTOR = HEAD**-0.5 * math.log2(math.e)
HIGH = 2.0**100
VMEM_MIB = 16


def contract_last(a, b):
    return lax.dot_general(a, b, (((1,), (1,)), ((), ())), preferred_element_type=jnp.float32)


def lane_sum(weights):
    parts = [weights[:, i : i + HEAD] for i in range(0, weights.shape[1], HEAD)]
    while len(parts) > 1:
        parts = [a + b for a, b in zip(parts[::2], parts[1::2])]
    return parts[0]


def own_masks(own_ref):
    ids = own_ref[2 * BLOCK :, :].astype(jnp.float32)
    key_ids = jnp.concatenate([ids[0:1, :], ids[1:2, :]], axis=1)
    key_ids = jnp.broadcast_to(key_ids, (BLOCK, BLOCK))
    query_ids = key_ids.T
    q_pos = lax.broadcasted_iota(jnp.int32, (BLOCK, BLOCK), 0)
    k_pos = lax.broadcasted_iota(jnp.int32, (BLOCK, BLOCK), 1)
    visible = (key_ids == query_ids) & (k_pos <= q_pos)
    in_first = (query_ids == key_ids[0:1, 0:1])[:, :HEAD]
    return visible, in_first


def add_own(q_ref, own_ref, shift_ref, l_ref, acc_ref):
    visible, in_first = own_masks(own_ref)
    keys = own_ref[:BLOCK, :]
    values = own_ref[BLOCK : 2 * BLOCK, :]
    for h in range(HEADS):
        rows = pl.ds(h * BLOCK, BLOCK)
        scores = contract_last(q_ref[:, h * HEAD : (h + 1) * HEAD], keys) * FACTOR
        scores = jnp.where(visible, scores, NEGATIVE)
        top = jnp.max(scores, axis=1, keepdims=True)
        weights = jnp.exp2(scores - top)
        l_ref[rows, :] = lane_sum(weights)
        acc_ref[rows, :] = jnp.dot(
            weights.astype(jnp.bfloat16), values, preferred_element_type=jnp.float32
        )
        shift_ref[rows, :] = jnp.where(
            in_first, jnp.broadcast_to(top, (BLOCK, HEAD)), -NEGATIVE
        )


def seen_rows(first_id, ids):
    ids = ids.astype(jnp.float32)
    return jnp.sum(jnp.where(ids == first_id, 1.0, 0.0)).astype(jnp.int32)


def gather(slots, counts, ok_ref, own_ref, k_buf, v_buf, part):
    first_id = own_ref[2 * BLOCK :, :].astype(jnp.float32)[0:1, 0:1]
    places = [(ref, k * SLOT) for ref, count in zip(slots, counts) for k in range(count)]
    seen = [seen_rows(first_id, ref[at + 2 * BLOCK : at + SLOT, :]) for ref, at in places]
    seen = [rows * ok_ref[i] for i, rows in enumerate(seen)]
    full = jnp.int32(0)
    partial = jnp.int32(0)
    for rows, (ref, at) in zip(seen, places):
        whole = rows == BLOCK

        @pl.when(whole)
        def _():
            to = pl.ds(pl.multiple_of(full * BLOCK, BLOCK), BLOCK)
            k_buf[to, :] = ref[at : at + BLOCK, :]
            v_buf[to, :] = ref[at + BLOCK : at + 2 * BLOCK, :]

        @pl.when((rows > 0) & (rows < BLOCK))
        def _():
            part[...] = ref[at : at + 2 * BLOCK, :]

        full = full + whole.astype(jnp.int32)
        partial = partial + jnp.where(whole, 0, rows)
    return full, partial


def add_blocks(full, partial, q_ref, shift_ref, l_ref, acc_ref, k_buf, v_buf, part):
    def attend(chunk, limit):
        at = pl.ds(pl.multiple_of(chunk * WIDE, WIDE), WIDE)
        keys, values = k_buf[at, :], v_buf[at, :]
        for h in range(0, HEADS, TOGETHER):
            rows = pl.ds(h * BLOCK, TOGETHER * BLOCK)
            some = [q_ref[:, i * HEAD : (i + 1) * HEAD] for i in range(h, h + TOGETHER)]
            scores = contract_last(jnp.concatenate(some, axis=0), keys) * FACTOR
            if limit is not None:
                scores = scores + limit
            shift = shift_ref[rows, :]
            weights = jnp.exp2(scores - jnp.concatenate([shift] * (WIDE // HEAD), axis=1))
            l_ref[rows, :] += lane_sum(weights)
            acc_ref[rows, :] += jnp.dot(
                weights.astype(jnp.bfloat16), values, preferred_element_type=jnp.float32
            )

    pairs = full // 2
    odd = full - 2 * pairs

    @pl.loop(0, pairs)
    def _(chunk):
        attend(chunk, None)

    @pl.when((odd > 0) | (partial > 0))
    def _():
        left = pl.ds(pl.multiple_of(pairs * WIDE, WIDE), BLOCK)
        right = pl.ds(pl.multiple_of(pairs * WIDE + BLOCK, BLOCK), BLOCK)
        none = jnp.zeros((BLOCK, HEAD), jnp.bfloat16)

        @pl.when(odd == 0)
        def _():
            k_buf[left, :] = none
            v_buf[left, :] = none

        @pl.when(partial > 0)
        def _():
            k_buf[right, :] = part[:BLOCK, :]
            v_buf[right, :] = part[BLOCK:, :]

        @pl.when(partial == 0)
        def _():
            k_buf[right, :] = none
            v_buf[right, :] = none

        k_pos = lax.broadcasted_iota(jnp.int32, (1, WIDE), 1)
        shown = ((k_pos < BLOCK) & (odd > 0)) | (k_pos >= WIDE - partial)
        attend(pairs, jnp.where(shown, 0.0, NEGATIVE))


def copies(pairs, sems):
    return [pltpu.make_async_copy(a, b, sems.at[i]) for i, (a, b) in enumerate(pairs)]


def run(moves):
    for move in moves:
        move.start()
    for move in moves:
        move.wait()


def first_kernel(counts, *refs):
    n = len(counts)
    ok_ref, q_hbm, own_ref = refs[:3]
    slots = refs[3 : 3 + n]
    shift_out, l_out, acc_out, q, shift, l_sum, acc_sum, k_buf, v_buf, part, sems = refs[3 + n :]
    fetch, *keep = copies(
        [(q_hbm, q), (shift, shift_out), (l_sum, l_out), (acc_sum, acc_out)], sems
    )
    fetch.start()
    full, partial = gather(slots, counts, ok_ref, own_ref, k_buf, v_buf, part)
    fetch.wait()
    add_own(q, own_ref, shift, l_sum, acc_sum)
    keep[0].start()
    add_blocks(full, partial, q, shift, l_sum, acc_sum, k_buf, v_buf, part)
    keep[1].start()
    keep[2].start()
    for move in keep:
        move.wait()


def more_kernel(counts, *refs):
    n = len(counts)
    ok_ref, q_hbm, own_ref, shift_in, l_in, acc_in = refs[:6]
    slots = refs[6 : 6 + n]
    l_sum, acc_sum, q, shift, k_buf, v_buf, part, sems = refs[6 + n :]
    moves = copies([(l_in, l_sum), (acc_in, acc_sum), (q_hbm, q), (shift_in, shift)], sems)
    for move in moves:
        move.start()
    full, partial = gather(slots, counts, ok_ref, own_ref, k_buf, v_buf, part)
    for move in moves:
        move.wait()
    add_blocks(full, partial, q, shift, l_sum, acc_sum, k_buf, v_buf, part)


def last_kernel(counts, all_counts, *refs):
    n, m = len(counts), len(all_counts)
    ok_ref, all_ok_ref, q, own_ref, shift, l_in, acc_in = refs[:7]
    slots, everything = refs[7 : 7 + n], refs[7 + n : 7 + n + m]
    out_ref, l_sum, acc_sum, k_buf, v_buf, part, store, top, sems = refs[7 + n + m :]
    full, partial = gather(slots, counts, ok_ref, own_ref, k_buf, v_buf, part)
    l_sum[...] = l_in[...]
    acc_sum[...] = acc_in[...]
    add_blocks(full, partial, q, shift, l_sum, acc_sum, k_buf, v_buf, part)
    most = jnp.zeros((BLOCK, 1), jnp.float32)
    for h in range(HEADS):
        rows = pl.ds(h * BLOCK, BLOCK)
        total = jnp.sum(l_sum[rows, :], axis=1, keepdims=True)
        most = jnp.where(total <= HIGH, most, 1.0)
        out_ref[:, h * HEAD : (h + 1) * HEAD] = (acc_sum[rows, :] * (1.0 / total)).astype(
            jnp.bfloat16
        )

    @pl.when(jnp.max(most) > 0.5)
    def _():
        at = 0
        for ref, count in zip(everything, all_counts):
            for k in range(count):
                run(copies([(ref.at[k * SLOT : (k + 1) * SLOT, :], store.at[at])], sems))
                at += 1
        with_maximum(at, all_ok_ref, q, own_ref, store, top, l_sum, acc_sum, out_ref)


def with_maximum(count, ok_ref, q_ref, own_ref, store, top, l_sum, acc_sum, out_ref):
    visible, in_first = own_masks(own_ref)
    first_id = own_ref[2 * BLOCK :, :].astype(jnp.float32)[0:1, 0:1]
    own_bias = jnp.where(visible, 0.0, NEGATIVE)

    def head(h, carry):
        q = q_ref[:, pl.ds(pl.multiple_of(h * HEAD, HEAD), HEAD)]
        scores = contract_last(q, own_ref[:BLOCK, :]) * FACTOR + own_bias
        first_top = jnp.max(scores, axis=1, keepdims=True)
        weights = jnp.exp2(scores - first_top)
        top[...] = jnp.where(in_first, jnp.broadcast_to(first_top, (BLOCK, HEAD)), -NEGATIVE)
        l_sum[:BLOCK, :] = lane_sum(weights)
        acc_sum[:BLOCK, :] = jnp.dot(
            weights.astype(jnp.bfloat16),
            own_ref[BLOCK : 2 * BLOCK, :],
            preferred_element_type=jnp.float32,
        )

        def block(j, carry):
            seen = seen_rows(first_id, store[j, 2 * BLOCK :, :]) * ok_ref[j]

            @pl.when(seen > 0)
            def _():
                k_pos = lax.broadcasted_iota(jnp.int32, (1, BLOCK), 1)
                limit = jnp.where(k_pos >= BLOCK - seen, 0.0, NEGATIVE)
                scores = contract_last(q, store[j, :BLOCK, :]) * FACTOR + limit
                old = top[...]
                new = jnp.maximum(old, jnp.max(scores, axis=1, keepdims=True))
                fade = jnp.exp2(old - new)
                weights = jnp.exp2(scores - new[:, 0:1])
                l_sum[:BLOCK, :] = l_sum[:BLOCK, :] * fade + lane_sum(weights)
                acc_sum[:BLOCK, :] = acc_sum[:BLOCK, :] * fade + jnp.dot(
                    weights.astype(jnp.bfloat16),
                    store[j, BLOCK : 2 * BLOCK, :],
                    preferred_element_type=jnp.float32,
                )
                top[...] = new

            return carry

        lax.fori_loop(0, count, block, 0)
        total = jnp.sum(l_sum[:BLOCK, :], axis=1, keepdims=True)
        out_ref[:, pl.ds(pl.multiple_of(h * HEAD, HEAD), HEAD)] = (
            acc_sum[:BLOCK, :] * (1.0 / total)
        ).astype(jnp.bfloat16)
        return carry

    lax.fori_loop(0, HEADS, head, 0)


VMEM = pl.BlockSpec(memory_space=pltpu.VMEM)
SMEM = pl.BlockSpec(memory_space=pltpu.SMEM)
HBM = pl.BlockSpec(memory_space=pltpu.HBM)
SUMS = jax.ShapeDtypeStruct((HEADS * BLOCK, HEAD), jnp.float32)
COST = pl.CostEstimate(flops=1, bytes_accessed=1, transcendentals=0)


def params(mib):
    return pltpu.CompilerParams(vmem_limit_bytes=mib * 1024 * 1024)


def buffers(blocks):
    rows = (blocks + blocks % 2 + 2) * BLOCK
    return [
        pltpu.VMEM((rows, HEAD), jnp.bfloat16),
        pltpu.VMEM((rows, HEAD), jnp.bfloat16),
        pltpu.VMEM((2 * BLOCK, HEAD), jnp.bfloat16),
    ]


QUERIES = pltpu.VMEM((BLOCK, HEADS * HEAD), jnp.bfloat16)
SUM = pltpu.VMEM(SUMS.shape, jnp.float32)
SEMS = pltpu.SemaphoreType.DMA((4,))


def in_hbm(*arrays):
    return [pltpu.with_memory_space_constraint(a, pltpu.HBM) for a in arrays]


def stack_ok(ok):
    return jnp.stack([jnp.asarray(o, jnp.int32) for o in ok])


def attend_first(q, own, arrays, ok):
    counts = [a.shape[0] // SLOT for a in arrays]
    return pl.pallas_call(
        functools.partial(first_kernel, counts),
        out_shape=[pltpu.HBM(SUMS.shape, SUMS.dtype)] * 3,
        in_specs=[SMEM, HBM, VMEM] + [VMEM] * len(arrays),
        out_specs=[HBM] * 3,
        scratch_shapes=[QUERIES] + [SUM] * 3 + buffers(sum(counts)) + [SEMS],
        compiler_params=params(VMEM_MIB), cost_estimate=COST, name="attend_first",
    )(stack_ok(ok), *in_hbm(q), own, *arrays)


def attend_more(state, q, own, arrays, ok):
    counts = [a.shape[0] // SLOT for a in arrays]
    sums = pl.pallas_call(
        functools.partial(more_kernel, counts),
        out_shape=[SUMS] * 2,
        in_specs=[SMEM, HBM, VMEM] + [HBM] * 3 + [VMEM] * len(arrays),
        out_specs=[VMEM] * 2,
        scratch_shapes=[QUERIES, SUM] + buffers(sum(counts)) + [SEMS],
        compiler_params=params(VMEM_MIB), cost_estimate=COST, name="attend_more",
    )(stack_ok(ok), *in_hbm(q), own, *in_hbm(*state), *arrays)
    return state[0], *sums


def attend_last(state, q, own, arrays, ok, everything, all_ok):
    counts = [a.shape[0] // SLOT for a in arrays]
    all_counts = [a.shape[0] // SLOT for a in everything]
    return pl.pallas_call(
        functools.partial(last_kernel, counts, all_counts),
        out_shape=jax.ShapeDtypeStruct((BLOCK, HEADS * HEAD), jnp.bfloat16),
        in_specs=[SMEM] * 2 + [VMEM] * 5 + [VMEM] * len(arrays)
        + [pl.BlockSpec(memory_space=pl.ANY)] * len(everything),
        out_specs=VMEM,
        scratch_shapes=[SUM] * 2 + buffers(sum(counts))
        + [
            pltpu.VMEM((sum(all_counts), SLOT, HEAD), jnp.bfloat16),
            pltpu.VMEM((BLOCK, HEAD), jnp.float32),
            SEMS,
        ],
        compiler_params=params(VMEM_MIB), cost_estimate=COST, name="attend_last",
    )(stack_ok(ok), stack_ok(all_ok), q, own, *state, *arrays, *everything)


def exchange(v, mask):
    return lax.ppermute(v, "ctx", [(i, i ^ mask) for i in range(NX * NZ)])


def along_x(v, steps):
    return lax.ppermute(v, "ctx", [(i, i + NZ * steps) for i in range((NX - steps) * NZ)])


def together(*arrays):
    return lax.optimization_barrier(arrays)


def per_device(queries, keys, values, doc_ids):
    z = lax.axis_index("ctx") % NZ
    bit = [(z >> b) & 1 for b in range(3)]
    one = jnp.int32(1)
    ids = (doc_ids + 1).astype(jnp.bfloat16).reshape(2, HEAD)
    ids = jnp.pad(ids, ((0, IDS - 2), (0, 0)))
    own = jnp.concatenate([keys, values, ids], axis=0)
    q = queries

    b0 = along_x(own, 1)
    c0 = along_x(own, 2)
    p2 = exchange(own, 2)
    p4 = exchange(own, 4)
    p4, p2 = together(p4, p2)

    near1 = exchange(jnp.concatenate([b0, jnp.where(bit[0] == 0, own, c0)]), 1)
    pair = jnp.concatenate([p2, p4])
    b24 = along_x(pair, 1)
    c24 = along_x(pair, 2)
    p6 = exchange(p4, 2)
    state = attend_first(q, own, [p4, p2, b0, c0], [bit[2], bit[1], one, one])
    state, p6, near1, b24, c24 = together(state, p6, near1, b24, c24)

    sent = [
        b24,
        jnp.where(bit[1] == 1, p2, c24[:SLOT]),
        jnp.where(bit[2] == 1, p4, c24[SLOT:]),
    ]
    sent, p6 = together(jnp.concatenate(sent), p6)
    near35 = exchange(sent, 1)
    b6 = along_x(p6, 1)
    c6 = along_x(p6, 2)
    b6, c6 = together(b6, c6)

    near7 = exchange(jnp.concatenate([b6, jnp.where(bit[2] == 1, p6, c6)]), 1)
    state = attend_more(
        state, q, own, [near1, b24, c24, p6, b6, c6], [one] * 6 + [bit[2]] + [one] * 2
    )
    arrays = [p2, p4, b0, c0, near1, b24, c24, p6, near35, b6, c6, near7]
    ok = [bit[1], bit[2]] + [one] * 8 + [bit[2]] + [one] * 8
    return attend_last(state, q, own, [near35, near7], [one] * 6, arrays, ok)


def solution(mesh):
    return jax.shard_map(
        per_device,
        mesh=mesh,
        in_specs=(
            P(("dp", "ctx"), "tp"),
            P(("dp", "ctx"), "tp"),
            P(("dp", "ctx"), "tp"),
            P(("dp", "ctx")),
        ),
        out_specs=P(("dp", "ctx"), "tp"),
        check_vma=False,
    )
```

```python
import functools
import math

import jax
import jax.numpy as jnp
from jax import lax
from jax.experimental import pallas as pl
from jax.experimental.pallas import tpu as pltpu
from jax.sharding import PartitionSpec as P

HEAD = 128
BLOCK = 256
HEADS = 8
TOGETHER = 4
IDS = 16
SLOT = 2 * BLOCK + IDS
WIDE = 2 * BLOCK
NX, NZ = 4, 8
NEGATIVE = -1e30
FACTOR = HEAD**-0.5 * math.log2(math.e)
HIGH = 2.0**100
VMEM_MIB = 16


def contract_last(a, b):
    return lax.dot_general(a, b, (((1,), (1,)), ((), ())), preferred_element_type=jnp.float32)


def lane_sum(weights):
    parts = [weights[:, i : i + HEAD] for i in range(0, weights.shape[1], HEAD)]
    while len(parts) > 1:
        parts = [a + b for a, b in zip(parts[::2], parts[1::2])]
    return parts[0]


def own_masks(own_ref):
    ids = own_ref[2 * BLOCK :, :].astype(jnp.float32)
    key_ids = jnp.concatenate([ids[0:1, :], ids[1:2, :]], axis=1)
    key_ids = jnp.broadcast_to(key_ids, (BLOCK, BLOCK))
    query_ids = key_ids.T
    q_pos = lax.broadcasted_iota(jnp.int32, (BLOCK, BLOCK), 0)
    k_pos = lax.broadcasted_iota(jnp.int32, (BLOCK, BLOCK), 1)
    visible = (key_ids == query_ids) & (k_pos <= q_pos)
    in_first = (query_ids == key_ids[0:1, 0:1])[:, :HEAD]
    return visible, in_first


def add_own(q_ref, own_ref, shift_ref, l_ref, acc_ref):
    visible, in_first = own_masks(own_ref)
    keys = own_ref[:BLOCK, :]
    values = own_ref[BLOCK : 2 * BLOCK, :]
    for h in range(HEADS):
        rows = pl.ds(h * BLOCK, BLOCK)
        scores = contract_last(q_ref[:, h * HEAD : (h + 1) * HEAD], keys) * FACTOR
        scores = jnp.where(visible, scores, NEGATIVE)
        top = jnp.max(scores, axis=1, keepdims=True)
        weights = jnp.exp2(scores - top)
        l_ref[rows, :] = lane_sum(weights)
        acc_ref[rows, :] = jnp.dot(
            weights.astype(jnp.bfloat16), values, preferred_element_type=jnp.float32
        )
        shift_ref[rows, :] = jnp.where(
            in_first, jnp.broadcast_to(top, (BLOCK, HEAD)), -NEGATIVE
        )


def seen_rows(first_id, ids):
    ids = ids.astype(jnp.float32)
    return jnp.sum(jnp.where(ids == first_id, 1.0, 0.0)).astype(jnp.int32)


def gather(slots, counts, ok_ref, own_ref, k_buf, v_buf, part):
    first_id = own_ref[2 * BLOCK :, :].astype(jnp.float32)[0:1, 0:1]
    places = [(ref, k * SLOT) for ref, count in zip(slots, counts) for k in range(count)]
    seen = [seen_rows(first_id, ref[at + 2 * BLOCK : at + SLOT, :]) for ref, at in places]
    seen = [rows * ok_ref[i] for i, rows in enumerate(seen)]
    full = jnp.int32(0)
    partial = jnp.int32(0)
    for rows, (ref, at) in zip(seen, places):
        whole = rows == BLOCK

        @pl.when(whole)
        def _():
            to = pl.ds(pl.multiple_of(full * BLOCK, BLOCK), BLOCK)
            k_buf[to, :] = ref[at : at + BLOCK, :]
            v_buf[to, :] = ref[at + BLOCK : at + 2 * BLOCK, :]

        @pl.when((rows > 0) & (rows < BLOCK))
        def _():
            part[...] = ref[at : at + 2 * BLOCK, :]

        full = full + whole.astype(jnp.int32)
        partial = partial + jnp.where(whole, 0, rows)
    return full, partial


def add_blocks(full, partial, q_ref, shift_ref, l_ref, acc_ref, k_buf, v_buf, part):
    def attend(chunk, limit):
        at = pl.ds(pl.multiple_of(chunk * WIDE, WIDE), WIDE)
        keys, values = k_buf[at, :], v_buf[at, :]
        for h in range(0, HEADS, TOGETHER):
            rows = pl.ds(h * BLOCK, TOGETHER * BLOCK)
            some = [q_ref[:, i * HEAD : (i + 1) * HEAD] for i in range(h, h + TOGETHER)]
            scores = contract_last(jnp.concatenate(some, axis=0), keys) * FACTOR
            if limit is not None:
                scores = scores + limit
            shift = shift_ref[rows, :]
            weights = jnp.exp2(scores - jnp.concatenate([shift] * (WIDE // HEAD), axis=1))
            l_ref[rows, :] += lane_sum(weights)
            acc_ref[rows, :] += jnp.dot(
                weights.astype(jnp.bfloat16), values, preferred_element_type=jnp.float32
            )

    pairs = full // 2
    odd = full - 2 * pairs

    @pl.loop(0, pairs)
    def _(chunk):
        attend(chunk, None)

    @pl.when((odd > 0) | (partial > 0))
    def _():
        left = pl.ds(pl.multiple_of(pairs * WIDE, WIDE), BLOCK)
        right = pl.ds(pl.multiple_of(pairs * WIDE + BLOCK, BLOCK), BLOCK)
        none = jnp.zeros((BLOCK, HEAD), jnp.bfloat16)

        @pl.when(odd == 0)
        def _():
            k_buf[left, :] = none
            v_buf[left, :] = none

        @pl.when(partial > 0)
        def _():
            k_buf[right, :] = part[:BLOCK, :]
            v_buf[right, :] = part[BLOCK:, :]

        @pl.when(partial == 0)
        def _():
            k_buf[right, :] = none
            v_buf[right, :] = none

        k_pos = lax.broadcasted_iota(jnp.int32, (1, WIDE), 1)
        shown = ((k_pos < BLOCK) & (odd > 0)) | (k_pos >= WIDE - partial)
        attend(pairs, jnp.where(shown, 0.0, NEGATIVE))


def copies(pairs, sems):
    return [pltpu.make_async_copy(a, b, sems.at[i]) for i, (a, b) in enumerate(pairs)]


def run(moves):
    for move in moves:
        move.start()
    for move in moves:
        move.wait()


def first_kernel(counts, *refs):
    n = len(counts)
    ok_ref, q_hbm, own_ref = refs[:3]
    slots = refs[3 : 3 + n]
    shift_out, l_out, acc_out, q, shift, l_sum, acc_sum, k_buf, v_buf, part, sems = refs[3 + n :]
    fetch, *keep = copies(
        [(q_hbm, q), (shift, shift_out), (l_sum, l_out), (acc_sum, acc_out)], sems
    )
    fetch.start()
    full, partial = gather(slots, counts, ok_ref, own_ref, k_buf, v_buf, part)
    fetch.wait()
    add_own(q, own_ref, shift, l_sum, acc_sum)
    keep[0].start()
    add_blocks(full, partial, q, shift, l_sum, acc_sum, k_buf, v_buf, part)
    keep[1].start()
    keep[2].start()
    for move in keep:
        move.wait()


def middle_kernel(counts, *refs):
    n = len(counts)
    ok_ref, q_hbm, own_ref, shift_in, l_in, acc_in = refs[:6]
    slots = refs[6 : 6 + n]
    l_out, acc_out, q, shift, l_sum, acc_sum, k_buf, v_buf, part, sems = refs[6 + n :]
    full, partial = gather(slots, counts, ok_ref, own_ref, k_buf, v_buf, part)

    @pl.when((full > 0) | (partial > 0))
    def _():
        run(copies([(q_hbm, q), (shift_in, shift), (l_in, l_sum), (acc_in, acc_sum)], sems))
        add_blocks(full, partial, q, shift, l_sum, acc_sum, k_buf, v_buf, part)
        run(copies([(l_sum, l_out), (acc_sum, acc_out)], sems))


def more_kernel(counts, *refs):
    n = len(counts)
    ok_ref, q_hbm, own_ref, shift_in, l_in, acc_in = refs[:6]
    slots = refs[6 : 6 + n]
    l_sum, acc_sum, q, shift, k_buf, v_buf, part, sems = refs[6 + n :]
    moves = copies([(l_in, l_sum), (acc_in, acc_sum), (q_hbm, q), (shift_in, shift)], sems)
    for move in moves:
        move.start()
    full, partial = gather(slots, counts, ok_ref, own_ref, k_buf, v_buf, part)
    for move in moves:
        move.wait()
    add_blocks(full, partial, q, shift, l_sum, acc_sum, k_buf, v_buf, part)


def last_kernel(counts, all_counts, *refs):
    n, m = len(counts), len(all_counts)
    ok_ref, all_ok_ref, q, own_ref, shift, l_in, acc_in = refs[:7]
    slots, everything = refs[7 : 7 + n], refs[7 + n : 7 + n + m]
    out_ref, l_sum, acc_sum, k_buf, v_buf, part, store, top, sems = refs[7 + n + m :]
    full, partial = gather(slots, counts, ok_ref, own_ref, k_buf, v_buf, part)
    l_sum[...] = l_in[...]
    acc_sum[...] = acc_in[...]
    add_blocks(full, partial, q, shift, l_sum, acc_sum, k_buf, v_buf, part)
    most = jnp.zeros((BLOCK, 1), jnp.float32)
    for h in range(HEADS):
        rows = pl.ds(h * BLOCK, BLOCK)
        total = jnp.sum(l_sum[rows, :], axis=1, keepdims=True)
        most = jnp.where(total <= HIGH, most, 1.0)
        out_ref[:, h * HEAD : (h + 1) * HEAD] = (acc_sum[rows, :] * (1.0 / total)).astype(
            jnp.bfloat16
        )

    @pl.when(jnp.max(most) > 0.5)
    def _():
        at = 0
        for ref, count in zip(everything, all_counts):
            for k in range(count):
                run(copies([(ref.at[k * SLOT : (k + 1) * SLOT, :], store.at[at])], sems))
                at += 1
        with_maximum(at, all_ok_ref, q, own_ref, store, top, l_sum, acc_sum, out_ref)


def with_maximum(count, ok_ref, q_ref, own_ref, store, top, l_sum, acc_sum, out_ref):
    visible, in_first = own_masks(own_ref)
    first_id = own_ref[2 * BLOCK :, :].astype(jnp.float32)[0:1, 0:1]
    own_bias = jnp.where(visible, 0.0, NEGATIVE)

    def head(h, carry):
        q = q_ref[:, pl.ds(pl.multiple_of(h * HEAD, HEAD), HEAD)]
        scores = contract_last(q, own_ref[:BLOCK, :]) * FACTOR + own_bias
        first_top = jnp.max(scores, axis=1, keepdims=True)
        weights = jnp.exp2(scores - first_top)
        top[...] = jnp.where(in_first, jnp.broadcast_to(first_top, (BLOCK, HEAD)), -NEGATIVE)
        l_sum[:BLOCK, :] = lane_sum(weights)
        acc_sum[:BLOCK, :] = jnp.dot(
            weights.astype(jnp.bfloat16),
            own_ref[BLOCK : 2 * BLOCK, :],
            preferred_element_type=jnp.float32,
        )

        def block(j, carry):
            seen = seen_rows(first_id, store[j, 2 * BLOCK :, :]) * ok_ref[j]

            @pl.when(seen > 0)
            def _():
                k_pos = lax.broadcasted_iota(jnp.int32, (1, BLOCK), 1)
                limit = jnp.where(k_pos >= BLOCK - seen, 0.0, NEGATIVE)
                scores = contract_last(q, store[j, :BLOCK, :]) * FACTOR + limit
                old = top[...]
                new = jnp.maximum(old, jnp.max(scores, axis=1, keepdims=True))
                fade = jnp.exp2(old - new)
                weights = jnp.exp2(scores - new[:, 0:1])
                l_sum[:BLOCK, :] = l_sum[:BLOCK, :] * fade + lane_sum(weights)
                acc_sum[:BLOCK, :] = acc_sum[:BLOCK, :] * fade + jnp.dot(
                    weights.astype(jnp.bfloat16),
                    store[j, BLOCK : 2 * BLOCK, :],
                    preferred_element_type=jnp.float32,
                )
                top[...] = new

            return carry

        lax.fori_loop(0, count, block, 0)
        total = jnp.sum(l_sum[:BLOCK, :], axis=1, keepdims=True)
        out_ref[:, pl.ds(pl.multiple_of(h * HEAD, HEAD), HEAD)] = (
            acc_sum[:BLOCK, :] * (1.0 / total)
        ).astype(jnp.bfloat16)
        return carry

    lax.fori_loop(0, HEADS, head, 0)


VMEM = pl.BlockSpec(memory_space=pltpu.VMEM)
SMEM = pl.BlockSpec(memory_space=pltpu.SMEM)
HBM = pl.BlockSpec(memory_space=pltpu.HBM)
SUMS = jax.ShapeDtypeStruct((HEADS * BLOCK, HEAD), jnp.float32)
COST = pl.CostEstimate(flops=1, bytes_accessed=1, transcendentals=0)


def params(mib):
    return pltpu.CompilerParams(vmem_limit_bytes=mib * 1024 * 1024)


def buffers(blocks):
    rows = (blocks + blocks % 2 + 2) * BLOCK
    return [
        pltpu.VMEM((rows, HEAD), jnp.bfloat16),
        pltpu.VMEM((rows, HEAD), jnp.bfloat16),
        pltpu.VMEM((2 * BLOCK, HEAD), jnp.bfloat16),
    ]


QUERIES = pltpu.VMEM((BLOCK, HEADS * HEAD), jnp.bfloat16)
SUM = pltpu.VMEM(SUMS.shape, jnp.float32)
SEMS = pltpu.SemaphoreType.DMA((4,))


def in_hbm(*arrays):
    return [pltpu.with_memory_space_constraint(a, pltpu.HBM) for a in arrays]


def stack_ok(ok):
    return jnp.stack([jnp.asarray(o, jnp.int32) for o in ok])


def attend_first(q, own, arrays, ok):
    counts = [a.shape[0] // SLOT for a in arrays]
    return pl.pallas_call(
        functools.partial(first_kernel, counts),
        out_shape=[pltpu.HBM(SUMS.shape, SUMS.dtype)] * 3,
        in_specs=[SMEM, HBM, VMEM] + [VMEM] * len(arrays),
        out_specs=[HBM] * 3,
        scratch_shapes=[QUERIES] + [SUM] * 3 + buffers(sum(counts)) + [SEMS],
        compiler_params=params(VMEM_MIB), cost_estimate=COST, name="attend_first",
    )(stack_ok(ok), *in_hbm(q), own, *arrays)


def attend_more(state, q, own, arrays, ok, final):
    counts = [a.shape[0] // SLOT for a in arrays]
    scratch = [QUERIES, SUM] if final else [QUERIES] + [SUM] * 3
    sums = pl.pallas_call(
        functools.partial(more_kernel if final else middle_kernel, counts),
        out_shape=[SUMS if final else pltpu.HBM(SUMS.shape, SUMS.dtype)] * 2,
        in_specs=[SMEM, HBM, VMEM] + [HBM] * 3 + [VMEM] * len(arrays),
        out_specs=[VMEM if final else HBM] * 2,
        scratch_shapes=scratch + buffers(sum(counts)) + [SEMS],
        input_output_aliases={} if final else {4: 0, 5: 1},
        compiler_params=params(VMEM_MIB), cost_estimate=COST,
        name="attend_more" if final else "attend_middle",
    )(stack_ok(ok), *in_hbm(q), own, *in_hbm(*state), *arrays)
    return state[0], *sums


def attend_last(state, q, own, arrays, ok, everything, all_ok):
    counts = [a.shape[0] // SLOT for a in arrays]
    all_counts = [a.shape[0] // SLOT for a in everything]
    return pl.pallas_call(
        functools.partial(last_kernel, counts, all_counts),
        out_shape=jax.ShapeDtypeStruct((BLOCK, HEADS * HEAD), jnp.bfloat16),
        in_specs=[SMEM] * 2 + [VMEM] * 5 + [VMEM] * len(arrays)
        + [pl.BlockSpec(memory_space=pl.ANY)] * len(everything),
        out_specs=VMEM,
        scratch_shapes=[SUM] * 2 + buffers(sum(counts))
        + [
            pltpu.VMEM((sum(all_counts), SLOT, HEAD), jnp.bfloat16),
            pltpu.VMEM((BLOCK, HEAD), jnp.float32),
            SEMS,
        ],
        compiler_params=params(VMEM_MIB), cost_estimate=COST, name="attend_last",
    )(stack_ok(ok), stack_ok(all_ok), q, own, *state, *arrays, *everything)


def exchange(v, mask):
    return lax.ppermute(v, "ctx", [(i, i ^ mask) for i in range(NX * NZ)])


def along_x(v, steps):
    return lax.ppermute(v, "ctx", [(i, i + NZ * steps) for i in range((NX - steps) * NZ)])


def together(*arrays):
    return lax.optimization_barrier(arrays)


def per_device(queries, keys, values, doc_ids):
    z = lax.axis_index("ctx") % NZ
    bit = [(z >> b) & 1 for b in range(3)]
    one = jnp.int32(1)
    ids = (doc_ids + 1).astype(jnp.bfloat16).reshape(2, HEAD)
    ids = jnp.pad(ids, ((0, IDS - 2), (0, 0)))
    own = jnp.concatenate([keys, values, ids], axis=0)
    q = queries

    b0 = along_x(own, 1)
    c0 = along_x(own, 2)
    p2 = exchange(own, 2)
    p4 = exchange(own, 4)
    c0, b0, p2, p4 = together(c0, b0, p2, p4)

    near1 = exchange(jnp.concatenate([b0, jnp.where(bit[0] == 0, own, c0)]), 1)
    pair = jnp.concatenate([p2, p4])
    b24 = along_x(pair, 1)
    c24 = along_x(pair, 2)
    p6 = exchange(p4, 2)
    state = attend_first(q, own, [p4, p2, b0, c0], [bit[2], bit[1], one, one])
    state, near1, c24, b24, p6 = together(state, near1, c24, b24, p6)

    sent = [
        b24,
        jnp.where(bit[1] == 1, p2, c24[:SLOT]),
        jnp.where(bit[2] == 1, p4, c24[SLOT:]),
    ]
    near35 = exchange(jnp.concatenate(sent), 1)
    b6 = along_x(p6, 1)
    c6 = along_x(p6, 2)
    state = attend_more(state, q, own, [near1, b24, c24, p6], [one] * 6 + [bit[2]], False)
    state, near35, b6, c6 = together(state, near35, b6, c6)

    near7 = exchange(jnp.concatenate([b6, jnp.where(bit[2] == 1, p6, c6)]), 1)
    state = attend_more(state, q, own, [near35, b6, c6], [one] * 6, True)
    arrays = [p2, p4, b0, c0, near1, b24, c24, p6, near35, b6, c6, near7]
    ok = [bit[1], bit[2]] + [one] * 8 + [bit[2]] + [one] * 8
    return attend_last(state, q, own, [near7], [one] * 2, arrays, ok)


def solution(mesh):
    return jax.shard_map(
        per_device,
        mesh=mesh,
        in_specs=(
            P(("dp", "ctx"), "tp"),
            P(("dp", "ctx"), "tp"),
            P(("dp", "ctx"), "tp"),
            P(("dp", "ctx")),
        ),
        out_specs=P(("dp", "ctx"), "tp"),
        check_vma=False,
    )
```

```python
import functools
import math

import jax
import jax.numpy as jnp
from jax import lax
from jax.experimental import pallas as pl
from jax.experimental.pallas import tpu as pltpu
from jax.sharding import PartitionSpec as P

HEAD = 128
BLOCK = 256
HEADS = 8
TOGETHER = 4
IDS = 16
SLOT = 2 * BLOCK + IDS
WIDE = 2 * BLOCK
NX, NZ = 4, 8
NEGATIVE = -1e30
FACTOR = HEAD**-0.5 * math.log2(math.e)
HIGH = 2.0**100
VMEM_MIB = 16


def contract_last(a, b):
    return lax.dot_general(a, b, (((1,), (1,)), ((), ())), preferred_element_type=jnp.float32)


def lane_sum(weights):
    parts = [weights[:, i : i + HEAD] for i in range(0, weights.shape[1], HEAD)]
    while len(parts) > 1:
        parts = [a + b for a, b in zip(parts[::2], parts[1::2])]
    return parts[0]


def own_masks(own_ref):
    ids = own_ref[2 * BLOCK :, :].astype(jnp.float32)
    key_ids = jnp.concatenate([ids[0:1, :], ids[1:2, :]], axis=1)
    key_ids = jnp.broadcast_to(key_ids, (BLOCK, BLOCK))
    query_ids = key_ids.T
    q_pos = lax.broadcasted_iota(jnp.int32, (BLOCK, BLOCK), 0)
    k_pos = lax.broadcasted_iota(jnp.int32, (BLOCK, BLOCK), 1)
    visible = (key_ids == query_ids) & (k_pos <= q_pos)
    in_first = (query_ids == key_ids[0:1, 0:1])[:, :HEAD]
    return visible, in_first


def add_own(q_ref, own_ref, shift_ref, l_ref, acc_ref):
    visible, in_first = own_masks(own_ref)
    keys = own_ref[:BLOCK, :]
    values = own_ref[BLOCK : 2 * BLOCK, :]
    for h in range(HEADS):
        rows = pl.ds(h * BLOCK, BLOCK)
        scores = contract_last(q_ref[:, h * HEAD : (h + 1) * HEAD], keys) * FACTOR
        scores = jnp.where(visible, scores, NEGATIVE)
        top = jnp.max(scores, axis=1, keepdims=True)
        weights = jnp.exp2(scores - top)
        l_ref[rows, :] = lane_sum(weights)
        acc_ref[rows, :] = jnp.dot(
            weights.astype(jnp.bfloat16), values, preferred_element_type=jnp.float32
        )
        shift_ref[rows, :] = jnp.where(
            in_first, jnp.broadcast_to(top, (BLOCK, HEAD)), -NEGATIVE
        )


def seen_rows(first_id, ids):
    ids = ids.astype(jnp.float32)
    return jnp.sum(jnp.where(ids == first_id, 1.0, 0.0)).astype(jnp.int32)


def gather(slots, counts, ok_ref, own_ref, k_buf, v_buf, part):
    first_id = own_ref[2 * BLOCK :, :].astype(jnp.float32)[0:1, 0:1]
    places = [(ref, k * SLOT) for ref, count in zip(slots, counts) for k in range(count)]
    seen = [seen_rows(first_id, ref[at + 2 * BLOCK : at + SLOT, :]) for ref, at in places]
    seen = [rows * ok_ref[i] for i, rows in enumerate(seen)]
    full = jnp.int32(0)
    partial = jnp.int32(0)
    for rows, (ref, at) in zip(seen, places):
        whole = rows == BLOCK

        @pl.when(whole)
        def _():
            to = pl.ds(pl.multiple_of(full * BLOCK, BLOCK), BLOCK)
            k_buf[to, :] = ref[at : at + BLOCK, :]
            v_buf[to, :] = ref[at + BLOCK : at + 2 * BLOCK, :]

        @pl.when((rows > 0) & (rows < BLOCK))
        def _():
            part[...] = ref[at : at + 2 * BLOCK, :]

        full = full + whole.astype(jnp.int32)
        partial = partial + jnp.where(whole, 0, rows)
    return full, partial


def add_blocks(full, partial, q_ref, shift_ref, l_ref, acc_ref, k_buf, v_buf, part):
    def attend(chunk, limit):
        at = pl.ds(pl.multiple_of(chunk * WIDE, WIDE), WIDE)
        keys, values = k_buf[at, :], v_buf[at, :]
        for h in range(0, HEADS, TOGETHER):
            rows = pl.ds(h * BLOCK, TOGETHER * BLOCK)
            some = [q_ref[:, i * HEAD : (i + 1) * HEAD] for i in range(h, h + TOGETHER)]
            scores = contract_last(jnp.concatenate(some, axis=0), keys) * FACTOR
            if limit is not None:
                scores = scores + limit
            shift = shift_ref[rows, :]
            weights = jnp.exp2(scores - jnp.concatenate([shift] * (WIDE // HEAD), axis=1))
            l_ref[rows, :] += lane_sum(weights)
            acc_ref[rows, :] += jnp.dot(
                weights.astype(jnp.bfloat16), values, preferred_element_type=jnp.float32
            )

    pairs = full // 2
    odd = full - 2 * pairs

    @pl.loop(0, pairs)
    def _(chunk):
        attend(chunk, None)

    @pl.when((odd > 0) | (partial > 0))
    def _():
        left = pl.ds(pl.multiple_of(pairs * WIDE, WIDE), BLOCK)
        right = pl.ds(pl.multiple_of(pairs * WIDE + BLOCK, BLOCK), BLOCK)
        none = jnp.zeros((BLOCK, HEAD), jnp.bfloat16)

        @pl.when(odd == 0)
        def _():
            k_buf[left, :] = none
            v_buf[left, :] = none

        @pl.when(partial > 0)
        def _():
            k_buf[right, :] = part[:BLOCK, :]
            v_buf[right, :] = part[BLOCK:, :]

        @pl.when(partial == 0)
        def _():
            k_buf[right, :] = none
            v_buf[right, :] = none

        k_pos = lax.broadcasted_iota(jnp.int32, (1, WIDE), 1)
        shown = ((k_pos < BLOCK) & (odd > 0)) | (k_pos >= WIDE - partial)
        attend(pairs, jnp.where(shown, 0.0, NEGATIVE))


def copies(pairs, sems):
    return [pltpu.make_async_copy(a, b, sems.at[i]) for i, (a, b) in enumerate(pairs)]


def run(moves):
    for move in moves:
        move.start()
    for move in moves:
        move.wait()


def first_kernel(counts, *refs):
    n = len(counts)
    ok_ref, q_hbm, own_ref = refs[:3]
    slots = refs[3 : 3 + n]
    shift_out, l_out, acc_out, q, shift, l_sum, acc_sum, k_buf, v_buf, part, sems = refs[3 + n :]
    fetch, *keep = copies(
        [(q_hbm, q), (shift, shift_out), (l_sum, l_out), (acc_sum, acc_out)], sems
    )
    fetch.start()
    full, partial = gather(slots, counts, ok_ref, own_ref, k_buf, v_buf, part)
    fetch.wait()
    add_own(q, own_ref, shift, l_sum, acc_sum)
    keep[0].start()
    add_blocks(full, partial, q, shift, l_sum, acc_sum, k_buf, v_buf, part)
    keep[1].start()
    keep[2].start()
    for move in keep:
        move.wait()


def more_kernel(counts, *refs):
    n = len(counts)
    ok_ref, q_hbm, own_ref, shift_in, l_in, acc_in = refs[:6]
    slots = refs[6 : 6 + n]
    l_sum, acc_sum, q, shift, k_buf, v_buf, part, sems = refs[6 + n :]
    moves = copies([(l_in, l_sum), (acc_in, acc_sum), (q_hbm, q), (shift_in, shift)], sems)
    moves[0].start()
    moves[1].start()
    full, partial = gather(slots, counts, ok_ref, own_ref, k_buf, v_buf, part)
    found = (full > 0) | (partial > 0)

    @pl.when(found)
    def _():
        run(moves[2:])

    moves[0].wait()
    moves[1].wait()
    add_blocks(full, partial, q, shift, l_sum, acc_sum, k_buf, v_buf, part)


def last_kernel(counts, all_counts, *refs):
    n, m = len(counts), len(all_counts)
    ok_ref, all_ok_ref, q, own_ref, shift, l_in, acc_in = refs[:7]
    slots, everything = refs[7 : 7 + n], refs[7 + n : 7 + n + m]
    out_ref, l_sum, acc_sum, k_buf, v_buf, part, store, top, sems = refs[7 + n + m :]
    full, partial = gather(slots, counts, ok_ref, own_ref, k_buf, v_buf, part)
    l_sum[...] = l_in[...]
    acc_sum[...] = acc_in[...]
    add_blocks(full, partial, q, shift, l_sum, acc_sum, k_buf, v_buf, part)
    most = jnp.zeros((BLOCK, 1), jnp.float32)
    for h in range(HEADS):
        rows = pl.ds(h * BLOCK, BLOCK)
        total = jnp.sum(l_sum[rows, :], axis=1, keepdims=True)
        most = jnp.where(total <= HIGH, most, 1.0)
        out_ref[:, h * HEAD : (h + 1) * HEAD] = (acc_sum[rows, :] * (1.0 / total)).astype(
            jnp.bfloat16
        )

    @pl.when(jnp.max(most) > 0.5)
    def _():
        at = 0
        for ref, count in zip(everything, all_counts):
            for k in range(count):
                run(copies([(ref.at[k * SLOT : (k + 1) * SLOT, :], store.at[at])], sems))
                at += 1
        with_maximum(at, all_ok_ref, q, own_ref, store, top, l_sum, acc_sum, out_ref)


def with_maximum(count, ok_ref, q_ref, own_ref, store, top, l_sum, acc_sum, out_ref):
    visible, in_first = own_masks(own_ref)
    first_id = own_ref[2 * BLOCK :, :].astype(jnp.float32)[0:1, 0:1]
    own_bias = jnp.where(visible, 0.0, NEGATIVE)

    def head(h, carry):
        q = q_ref[:, pl.ds(pl.multiple_of(h * HEAD, HEAD), HEAD)]
        scores = contract_last(q, own_ref[:BLOCK, :]) * FACTOR + own_bias
        first_top = jnp.max(scores, axis=1, keepdims=True)
        weights = jnp.exp2(scores - first_top)
        top[...] = jnp.where(in_first, jnp.broadcast_to(first_top, (BLOCK, HEAD)), -NEGATIVE)
        l_sum[:BLOCK, :] = lane_sum(weights)
        acc_sum[:BLOCK, :] = jnp.dot(
            weights.astype(jnp.bfloat16),
            own_ref[BLOCK : 2 * BLOCK, :],
            preferred_element_type=jnp.float32,
        )

        def block(j, carry):
            seen = seen_rows(first_id, store[j, 2 * BLOCK :, :]) * ok_ref[j]

            @pl.when(seen > 0)
            def _():
                k_pos = lax.broadcasted_iota(jnp.int32, (1, BLOCK), 1)
                limit = jnp.where(k_pos >= BLOCK - seen, 0.0, NEGATIVE)
                scores = contract_last(q, store[j, :BLOCK, :]) * FACTOR + limit
                old = top[...]
                new = jnp.maximum(old, jnp.max(scores, axis=1, keepdims=True))
                fade = jnp.exp2(old - new)
                weights = jnp.exp2(scores - new[:, 0:1])
                l_sum[:BLOCK, :] = l_sum[:BLOCK, :] * fade + lane_sum(weights)
                acc_sum[:BLOCK, :] = acc_sum[:BLOCK, :] * fade + jnp.dot(
                    weights.astype(jnp.bfloat16),
                    store[j, BLOCK : 2 * BLOCK, :],
                    preferred_element_type=jnp.float32,
                )
                top[...] = new

            return carry

        lax.fori_loop(0, count, block, 0)
        total = jnp.sum(l_sum[:BLOCK, :], axis=1, keepdims=True)
        out_ref[:, pl.ds(pl.multiple_of(h * HEAD, HEAD), HEAD)] = (
            acc_sum[:BLOCK, :] * (1.0 / total)
        ).astype(jnp.bfloat16)
        return carry

    lax.fori_loop(0, HEADS, head, 0)


VMEM = pl.BlockSpec(memory_space=pltpu.VMEM)
SMEM = pl.BlockSpec(memory_space=pltpu.SMEM)
HBM = pl.BlockSpec(memory_space=pltpu.HBM)
SUMS = jax.ShapeDtypeStruct((HEADS * BLOCK, HEAD), jnp.float32)
COST = pl.CostEstimate(flops=1, bytes_accessed=1, transcendentals=0)


def params(mib):
    return pltpu.CompilerParams(vmem_limit_bytes=mib * 1024 * 1024)


def buffers(blocks):
    rows = (blocks + blocks % 2 + 2) * BLOCK
    return [
        pltpu.VMEM((rows, HEAD), jnp.bfloat16),
        pltpu.VMEM((rows, HEAD), jnp.bfloat16),
        pltpu.VMEM((2 * BLOCK, HEAD), jnp.bfloat16),
    ]


QUERIES = pltpu.VMEM((BLOCK, HEADS * HEAD), jnp.bfloat16)
SUM = pltpu.VMEM(SUMS.shape, jnp.float32)
SEMS = pltpu.SemaphoreType.DMA((4,))


def in_hbm(*arrays):
    return [pltpu.with_memory_space_constraint(a, pltpu.HBM) for a in arrays]


def stack_ok(ok):
    return jnp.stack([jnp.asarray(o, jnp.int32) for o in ok])


def attend_first(q, own, arrays, ok):
    counts = [a.shape[0] // SLOT for a in arrays]
    return pl.pallas_call(
        functools.partial(first_kernel, counts),
        out_shape=[pltpu.HBM(SUMS.shape, SUMS.dtype)] * 3,
        in_specs=[SMEM, HBM, VMEM] + [VMEM] * len(arrays),
        out_specs=[HBM] * 3,
        scratch_shapes=[QUERIES] + [SUM] * 3 + buffers(sum(counts)) + [SEMS],
        compiler_params=params(VMEM_MIB), cost_estimate=COST, name="attend_first",
    )(stack_ok(ok), *in_hbm(q), own, *arrays)


def attend_more(state, q, own, arrays, ok, place):
    counts = [a.shape[0] // SLOT for a in arrays]
    shift, *sums = state
    if place is HBM:
        sums = in_hbm(*sums)
    sums = pl.pallas_call(
        functools.partial(more_kernel, counts),
        out_shape=[SUMS] * 2,
        in_specs=[SMEM, HBM, VMEM, HBM] + [place] * 2 + [VMEM] * len(arrays),
        out_specs=[VMEM] * 2,
        scratch_shapes=[QUERIES, SUM] + buffers(sum(counts)) + [SEMS],
        compiler_params=params(VMEM_MIB), cost_estimate=COST, name="attend_more",
    )(stack_ok(ok), *in_hbm(q), own, *in_hbm(shift), *sums, *arrays)
    return shift, *sums


def attend_last(state, q, own, arrays, ok, everything, all_ok):
    counts = [a.shape[0] // SLOT for a in arrays]
    all_counts = [a.shape[0] // SLOT for a in everything]
    return pl.pallas_call(
        functools.partial(last_kernel, counts, all_counts),
        out_shape=jax.ShapeDtypeStruct((BLOCK, HEADS * HEAD), jnp.bfloat16),
        in_specs=[SMEM] * 2 + [VMEM] * 5 + [VMEM] * len(arrays)
        + [pl.BlockSpec(memory_space=pl.ANY)] * len(everything),
        out_specs=VMEM,
        scratch_shapes=[SUM] * 2 + buffers(sum(counts))
        + [
            pltpu.VMEM((sum(all_counts), SLOT, HEAD), jnp.bfloat16),
            pltpu.VMEM((BLOCK, HEAD), jnp.float32),
            SEMS,
        ],
        compiler_params=params(VMEM_MIB), cost_estimate=COST, name="attend_last",
    )(stack_ok(ok), stack_ok(all_ok), q, own, *state, *arrays, *everything)


def exchange(v, mask):
    return lax.ppermute(v, "ctx", [(i, i ^ mask) for i in range(NX * NZ)])


def along_x(v, steps):
    return lax.ppermute(v, "ctx", [(i, i + NZ * steps) for i in range((NX - steps) * NZ)])


def together(*arrays):
    return lax.optimization_barrier(arrays)


def per_device(queries, keys, values, doc_ids):
    z = lax.axis_index("ctx") % NZ
    bit = [(z >> b) & 1 for b in range(3)]
    one = jnp.int32(1)
    ids = (doc_ids + 1).astype(jnp.bfloat16).reshape(2, HEAD)
    ids = jnp.pad(ids, ((0, IDS - 2), (0, 0)))
    own = jnp.concatenate([keys, values, ids], axis=0)
    q = queries

    b0 = along_x(own, 1)
    c0 = along_x(own, 2)
    p2 = exchange(own, 2)
    p4 = exchange(own, 4)
    p4, p2, b0, c0 = together(p4, p2, b0, c0)

    near1 = exchange(jnp.concatenate([b0, jnp.where(bit[0] == 0, own, c0)]), 1)
    pair = jnp.concatenate([p2, p4])
    p6 = exchange(p4, 2)
    b24 = along_x(pair, 1)
    c24 = along_x(pair, 2)
    state = attend_first(q, own, [p4, p2, b0, c0], [bit[2], bit[1], one, one])
    state, p6 = together(state, p6)

    b6 = along_x(p6, 1)
    c6 = along_x(p6, 2)
    state, b24, c24 = together(state, b24, c24)

    sent = [
        b24,
        jnp.where(bit[1] == 1, p2, c24[:SLOT]),
        jnp.where(bit[2] == 1, p4, c24[SLOT:]),
    ]
    sent = jnp.concatenate(sent)
    near35 = exchange(sent, 1)
    b6, c6, sent = together(b6, c6, sent)

    near7 = exchange(jnp.concatenate([b6, jnp.where(bit[2] == 1, p6, c6)]), 1)
    state = attend_more(
        state, q, own, [near1, b24, c24, p6, b6, c6], [one] * 6 + [bit[2]] + [one] * 2, HBM
    )
    state = attend_more(state, q, own, [near35], [one] * 4, VMEM)
    arrays = [p2, p4, b0, c0, near1, b24, c24, p6, near35, b6, c6, near7]
    ok = [bit[1], bit[2]] + [one] * 8 + [bit[2]] + [one] * 8
    return attend_last(state, q, own, [near7], [one] * 2, arrays, ok)


def solution(mesh):
    return jax.shard_map(
        per_device,
        mesh=mesh,
        in_specs=(
            P(("dp", "ctx"), "tp"),
            P(("dp", "ctx"), "tp"),
            P(("dp", "ctx"), "tp"),
            P(("dp", "ctx")),
        ),
        out_specs=P(("dp", "ctx"), "tp"),
        check_vma=False,
    )
```

```python
import functools
import math

import jax
import jax.numpy as jnp
from jax import lax
from jax.experimental import pallas as pl
from jax.experimental.pallas import tpu as pltpu
from jax.sharding import PartitionSpec as P

HEAD = 128
BLOCK = 256
HEADS = 8
TOGETHER = 4
IDS = 16
SLOT = 2 * BLOCK + IDS
WIDE = 2 * BLOCK
NX, NZ = 4, 8
NEGATIVE = -1e30
FACTOR = HEAD**-0.5 * math.log2(math.e)
HIGH = 2.0**100
VMEM_MIB = 16


def contract_last(a, b):
    return lax.dot_general(a, b, (((1,), (1,)), ((), ())), preferred_element_type=jnp.float32)


def lane_sum(weights):
    parts = [weights[:, i : i + HEAD] for i in range(0, weights.shape[1], HEAD)]
    while len(parts) > 1:
        parts = [a + b for a, b in zip(parts[::2], parts[1::2])]
    return parts[0]


def own_masks(own_ref):
    ids = own_ref[2 * BLOCK :, :].astype(jnp.float32)
    key_ids = jnp.concatenate([ids[0:1, :], ids[1:2, :]], axis=1)
    key_ids = jnp.broadcast_to(key_ids, (BLOCK, BLOCK))
    query_ids = key_ids.T
    q_pos = lax.broadcasted_iota(jnp.int32, (BLOCK, BLOCK), 0)
    k_pos = lax.broadcasted_iota(jnp.int32, (BLOCK, BLOCK), 1)
    visible = (key_ids == query_ids) & (k_pos <= q_pos)
    in_first = (query_ids == key_ids[0:1, 0:1])[:, :HEAD]
    return visible, in_first


def add_own(q_ref, own_ref, shift_ref, l_ref, acc_ref):
    visible, in_first = own_masks(own_ref)
    keys = own_ref[:BLOCK, :]
    values = own_ref[BLOCK : 2 * BLOCK, :]
    for h in range(HEADS):
        rows = pl.ds(h * BLOCK, BLOCK)
        scores = contract_last(q_ref[:, h * HEAD : (h + 1) * HEAD], keys) * FACTOR
        scores = jnp.where(visible, scores, NEGATIVE)
        top = jnp.max(scores, axis=1, keepdims=True)
        weights = jnp.exp2(scores - top)
        l_ref[rows, :] = lane_sum(weights)
        acc_ref[rows, :] = jnp.dot(
            weights.astype(jnp.bfloat16), values, preferred_element_type=jnp.float32
        )
        shift_ref[rows, :] = jnp.where(
            in_first, jnp.broadcast_to(top, (BLOCK, HEAD)), -NEGATIVE
        )


def seen_rows(first_id, ids):
    ids = ids.astype(jnp.float32)
    return jnp.sum(jnp.where(ids == first_id, 1.0, 0.0)).astype(jnp.int32)


def gather(slots, counts, ok_ref, own_ref, k_buf, v_buf, part):
    first_id = own_ref[2 * BLOCK :, :].astype(jnp.float32)[0:1, 0:1]
    places = [(ref, k * SLOT) for ref, count in zip(slots, counts) for k in range(count)]
    seen = [seen_rows(first_id, ref[at + 2 * BLOCK : at + SLOT, :]) for ref, at in places]
    seen = [rows * ok_ref[i] for i, rows in enumerate(seen)]
    full = jnp.int32(0)
    partial = jnp.int32(0)
    for rows, (ref, at) in zip(seen, places):
        whole = rows == BLOCK

        @pl.when(whole)
        def _():
            to = pl.ds(pl.multiple_of(full * BLOCK, BLOCK), BLOCK)
            k_buf[to, :] = ref[at : at + BLOCK, :]
            v_buf[to, :] = ref[at + BLOCK : at + 2 * BLOCK, :]

        @pl.when((rows > 0) & (rows < BLOCK))
        def _():
            part[...] = ref[at : at + 2 * BLOCK, :]

        full = full + whole.astype(jnp.int32)
        partial = partial + jnp.where(whole, 0, rows)
    return full, partial


def add_blocks(full, partial, q_ref, shift_ref, l_ref, acc_ref, k_buf, v_buf, part):
    def attend(chunk, limit):
        at = pl.ds(pl.multiple_of(chunk * WIDE, WIDE), WIDE)
        keys, values = k_buf[at, :], v_buf[at, :]
        for h in range(0, HEADS, TOGETHER):
            rows = pl.ds(h * BLOCK, TOGETHER * BLOCK)
            some = [q_ref[:, i * HEAD : (i + 1) * HEAD] for i in range(h, h + TOGETHER)]
            scores = contract_last(jnp.concatenate(some, axis=0), keys) * FACTOR
            if limit is not None:
                scores = scores + limit
            shift = shift_ref[rows, :]
            weights = jnp.exp2(scores - jnp.concatenate([shift] * (WIDE // HEAD), axis=1))
            l_ref[rows, :] += lane_sum(weights)
            acc_ref[rows, :] += jnp.dot(
                weights.astype(jnp.bfloat16), values, preferred_element_type=jnp.float32
            )

    pairs = full // 2
    odd = full - 2 * pairs

    @pl.loop(0, pairs)
    def _(chunk):
        attend(chunk, None)

    @pl.when((odd > 0) | (partial > 0))
    def _():
        left = pl.ds(pl.multiple_of(pairs * WIDE, WIDE), BLOCK)
        right = pl.ds(pl.multiple_of(pairs * WIDE + BLOCK, BLOCK), BLOCK)
        none = jnp.zeros((BLOCK, HEAD), jnp.bfloat16)

        @pl.when(odd == 0)
        def _():
            k_buf[left, :] = none
            v_buf[left, :] = none

        @pl.when(partial > 0)
        def _():
            k_buf[right, :] = part[:BLOCK, :]
            v_buf[right, :] = part[BLOCK:, :]

        @pl.when(partial == 0)
        def _():
            k_buf[right, :] = none
            v_buf[right, :] = none

        k_pos = lax.broadcasted_iota(jnp.int32, (1, WIDE), 1)
        shown = ((k_pos < BLOCK) & (odd > 0)) | (k_pos >= WIDE - partial)
        attend(pairs, jnp.where(shown, 0.0, NEGATIVE))


def copies(pairs, sems):
    return [pltpu.make_async_copy(a, b, sems.at[i]) for i, (a, b) in enumerate(pairs)]


def run(moves):
    for move in moves:
        move.start()
    for move in moves:
        move.wait()


def first_kernel(counts, *refs):
    n = len(counts)
    ok_ref, q_hbm, own_ref = refs[:3]
    slots = refs[3 : 3 + n]
    shift_out, l_out, acc_out, q, shift, l_sum, acc_sum, k_buf, v_buf, part, sems = refs[3 + n :]
    fetch, *keep = copies(
        [(q_hbm, q), (shift, shift_out), (l_sum, l_out), (acc_sum, acc_out)], sems
    )
    fetch.start()
    full, partial = gather(slots, counts, ok_ref, own_ref, k_buf, v_buf, part)
    fetch.wait()
    add_own(q, own_ref, shift, l_sum, acc_sum)
    keep[0].start()
    add_blocks(full, partial, q, shift, l_sum, acc_sum, k_buf, v_buf, part)
    keep[1].start()
    keep[2].start()
    for move in keep:
        move.wait()


def more_kernel(counts, *refs):
    n = len(counts)
    ok_ref, q_hbm, own_ref, shift_in, l_in, acc_in = refs[:6]
    slots = refs[6 : 6 + n]
    l_sum, acc_sum, q, shift, k_buf, v_buf, part, sems = refs[6 + n :]
    moves = copies([(q_hbm, q), (shift_in, shift), (l_in, l_sum), (acc_in, acc_sum)], sems)
    for move in moves:
        move.start()
    full, partial = gather(slots, counts, ok_ref, own_ref, k_buf, v_buf, part)
    for move in moves:
        move.wait()
    add_blocks(full, partial, q, shift, l_sum, acc_sum, k_buf, v_buf, part)


def last_kernel(counts, all_counts, *refs):
    n, m = len(counts), len(all_counts)
    ok_ref, all_ok_ref, q, own_ref, shift, l_in, acc_in = refs[:7]
    slots, everything = refs[7 : 7 + n], refs[7 + n : 7 + n + m]
    out_ref, l_sum, acc_sum, k_buf, v_buf, part, store, top, sems = refs[7 + n + m :]
    full, partial = gather(slots, counts, ok_ref, own_ref, k_buf, v_buf, part)
    l_sum[...] = l_in[...]
    acc_sum[...] = acc_in[...]
    add_blocks(full, partial, q, shift, l_sum, acc_sum, k_buf, v_buf, part)
    most = jnp.zeros((BLOCK, 1), jnp.float32)
    for h in range(HEADS):
        rows = pl.ds(h * BLOCK, BLOCK)
        total = jnp.sum(l_sum[rows, :], axis=1, keepdims=True)
        most = jnp.where(total <= HIGH, most, 1.0)
        out_ref[:, h * HEAD : (h + 1) * HEAD] = (acc_sum[rows, :] * (1.0 / total)).astype(
            jnp.bfloat16
        )

    @pl.when(jnp.max(most) > 0.5)
    def _():
        at = 0
        for ref, count in zip(everything, all_counts):
            for k in range(count):
                run(copies([(ref.at[k * SLOT : (k + 1) * SLOT, :], store.at[at])], sems))
                at += 1
        with_maximum(at, all_ok_ref, q, own_ref, store, top, l_sum, acc_sum, out_ref)


def with_maximum(count, ok_ref, q_ref, own_ref, store, top, l_sum, acc_sum, out_ref):
    visible, in_first = own_masks(own_ref)
    first_id = own_ref[2 * BLOCK :, :].astype(jnp.float32)[0:1, 0:1]
    own_bias = jnp.where(visible, 0.0, NEGATIVE)

    def head(h, carry):
        q = q_ref[:, pl.ds(pl.multiple_of(h * HEAD, HEAD), HEAD)]
        scores = contract_last(q, own_ref[:BLOCK, :]) * FACTOR + own_bias
        first_top = jnp.max(scores, axis=1, keepdims=True)
        weights = jnp.exp2(scores - first_top)
        top[...] = jnp.where(in_first, jnp.broadcast_to(first_top, (BLOCK, HEAD)), -NEGATIVE)
        l_sum[:BLOCK, :] = lane_sum(weights)
        acc_sum[:BLOCK, :] = jnp.dot(
            weights.astype(jnp.bfloat16),
            own_ref[BLOCK : 2 * BLOCK, :],
            preferred_element_type=jnp.float32,
        )

        def block(j, carry):
            seen = seen_rows(first_id, store[j, 2 * BLOCK :, :]) * ok_ref[j]

            @pl.when(seen > 0)
            def _():
                k_pos = lax.broadcasted_iota(jnp.int32, (1, BLOCK), 1)
                limit = jnp.where(k_pos >= BLOCK - seen, 0.0, NEGATIVE)
                scores = contract_last(q, store[j, :BLOCK, :]) * FACTOR + limit
                old = top[...]
                new = jnp.maximum(old, jnp.max(scores, axis=1, keepdims=True))
                fade = jnp.exp2(old - new)
                weights = jnp.exp2(scores - new[:, 0:1])
                l_sum[:BLOCK, :] = l_sum[:BLOCK, :] * fade + lane_sum(weights)
                acc_sum[:BLOCK, :] = acc_sum[:BLOCK, :] * fade + jnp.dot(
                    weights.astype(jnp.bfloat16),
                    store[j, BLOCK : 2 * BLOCK, :],
                    preferred_element_type=jnp.float32,
                )
                top[...] = new

            return carry

        lax.fori_loop(0, count, block, 0)
        total = jnp.sum(l_sum[:BLOCK, :], axis=1, keepdims=True)
        out_ref[:, pl.ds(pl.multiple_of(h * HEAD, HEAD), HEAD)] = (
            acc_sum[:BLOCK, :] * (1.0 / total)
        ).astype(jnp.bfloat16)
        return carry

    lax.fori_loop(0, HEADS, head, 0)


VMEM = pl.BlockSpec(memory_space=pltpu.VMEM)
SMEM = pl.BlockSpec(memory_space=pltpu.SMEM)
HBM = pl.BlockSpec(memory_space=pltpu.HBM)
SUMS = jax.ShapeDtypeStruct((HEADS * BLOCK, HEAD), jnp.float32)
COST = pl.CostEstimate(flops=1, bytes_accessed=1, transcendentals=0)


def params(mib):
    return pltpu.CompilerParams(vmem_limit_bytes=mib * 1024 * 1024)


def buffers(blocks):
    rows = (blocks + blocks % 2 + 2) * BLOCK
    return [
        pltpu.VMEM((rows, HEAD), jnp.bfloat16),
        pltpu.VMEM((rows, HEAD), jnp.bfloat16),
        pltpu.VMEM((2 * BLOCK, HEAD), jnp.bfloat16),
    ]


QUERIES = pltpu.VMEM((BLOCK, HEADS * HEAD), jnp.bfloat16)
SUM = pltpu.VMEM(SUMS.shape, jnp.float32)
SEMS = pltpu.SemaphoreType.DMA((4,))


def in_hbm(*arrays):
    return [pltpu.with_memory_space_constraint(a, pltpu.HBM) for a in arrays]


def stack_ok(ok):
    return jnp.stack([jnp.asarray(o, jnp.int32) for o in ok])


def attend_first(q, own, arrays, ok):
    counts = [a.shape[0] // SLOT for a in arrays]
    return pl.pallas_call(
        functools.partial(first_kernel, counts),
        out_shape=[pltpu.HBM(SUMS.shape, SUMS.dtype)] * 3,
        in_specs=[SMEM, HBM, VMEM] + [VMEM] * len(arrays),
        out_specs=[HBM] * 3,
        scratch_shapes=[QUERIES] + [SUM] * 3 + buffers(sum(counts)) + [SEMS],
        compiler_params=params(VMEM_MIB), cost_estimate=COST, name="attend_first",
    )(stack_ok(ok), *in_hbm(q), own, *arrays)


def attend_more(state, q, own, arrays, ok):
    counts = [a.shape[0] // SLOT for a in arrays]
    sums = pl.pallas_call(
        functools.partial(more_kernel, counts),
        out_shape=[SUMS] * 2,
        in_specs=[SMEM, HBM, VMEM] + [HBM] * 3 + [VMEM] * len(arrays),
        out_specs=[VMEM] * 2,
        scratch_shapes=[QUERIES, SUM] + buffers(sum(counts)) + [SEMS],
        compiler_params=params(VMEM_MIB), cost_estimate=COST, name="attend_more",
    )(stack_ok(ok), *in_hbm(q), own, *in_hbm(*state), *arrays)
    return state[0], *sums


def attend_last(state, q, own, arrays, ok, everything, all_ok):
    counts = [a.shape[0] // SLOT for a in arrays]
    all_counts = [a.shape[0] // SLOT for a in everything]
    return pl.pallas_call(
        functools.partial(last_kernel, counts, all_counts),
        out_shape=jax.ShapeDtypeStruct((BLOCK, HEADS * HEAD), jnp.bfloat16),
        in_specs=[SMEM] * 2 + [VMEM] * 5 + [VMEM] * len(arrays)
        + [pl.BlockSpec(memory_space=pl.ANY)] * len(everything),
        out_specs=VMEM,
        scratch_shapes=[SUM] * 2 + buffers(sum(counts))
        + [
            pltpu.VMEM((sum(all_counts), SLOT, HEAD), jnp.bfloat16),
            pltpu.VMEM((BLOCK, HEAD), jnp.float32),
            SEMS,
        ],
        compiler_params=params(VMEM_MIB), cost_estimate=COST, name="attend_last",
    )(stack_ok(ok), stack_ok(all_ok), q, own, *state, *arrays, *everything)


def exchange(v, mask):
    return lax.ppermute(v, "ctx", [(i, i ^ mask) for i in range(NX * NZ)])


def along_x(v, steps):
    return lax.ppermute(v, "ctx", [(i, i + NZ * steps) for i in range((NX - steps) * NZ)])


def together(*arrays):
    return lax.optimization_barrier(arrays)


def per_device(queries, keys, values, doc_ids):
    z = lax.axis_index("ctx") % NZ
    bit = [(z >> b) & 1 for b in range(3)]
    one = jnp.int32(1)
    ids = (doc_ids + 1).astype(jnp.bfloat16).reshape(2, HEAD)
    ids = jnp.pad(ids, ((0, IDS - 2), (0, 0)))
    (own,) = together(jnp.concatenate([keys, values, ids], axis=0))
    q = queries

    b0 = along_x(own, 1)
    c0 = along_x(own, 2)
    p2 = exchange(own, 2)
    p4 = exchange(own, 4)
    c0, b0, p2, p4 = together(c0, b0, p2, p4)

    near1 = exchange(jnp.concatenate([b0, jnp.where(bit[0] == 0, own, c0)]), 1)
    pair = jnp.concatenate([p2, p4])
    p6 = exchange(p4, 2)
    b24 = along_x(pair, 1)
    c24 = along_x(pair, 2)
    state = attend_first(q, own, [p4, p2, b0, c0], [bit[2], bit[1], one, one])
    state, p6 = together(state, p6)

    b6 = along_x(p6, 1)
    c6 = along_x(p6, 2)
    state, b24, c24 = together(state, b24, c24)

    sent = [
        b24,
        jnp.where(bit[1] == 1, p2, c24[:SLOT]),
        jnp.where(bit[2] == 1, p4, c24[SLOT:]),
    ]
    sent = jnp.concatenate(sent)
    near35 = exchange(sent, 1)
    b6, c6, sent = together(b6, c6, sent)

    near7 = exchange(jnp.concatenate([b6, jnp.where(bit[2] == 1, p6, c6)]), 1)
    state = attend_more(
        state, q, own, [near1, b24, c24, p6, b6, c6], [one] * 6 + [bit[2]] + [one] * 2
    )
    arrays = [p2, p4, b0, c0, near1, b24, c24, p6, near35, b6, c6, near7]
    ok = [bit[1], bit[2]] + [one] * 8 + [bit[2]] + [one] * 8
    return attend_last(state, q, own, [near35, near7], [one] * 6, arrays, ok)


def solution(mesh):
    return jax.shard_map(
        per_device,
        mesh=mesh,
        in_specs=(
            P(("dp", "ctx"), "tp"),
            P(("dp", "ctx"), "tp"),
            P(("dp", "ctx"), "tp"),
            P(("dp", "ctx")),
        ),
        out_specs=P(("dp", "ctx"), "tp"),
        check_vma=False,
    )
```

```python
import functools
import math

import jax
import jax.numpy as jnp
from jax import lax
from jax.experimental import pallas as pl
from jax.experimental.pallas import tpu as pltpu
from jax.sharding import PartitionSpec as P

HEAD = 128
BLOCK = 256
HEADS = 8
TOGETHER = 4
IDS = 16
SLOT = 2 * BLOCK + IDS
WIDE = 2 * BLOCK
NX, NZ = 4, 8
NEGATIVE = -1e30
FACTOR = HEAD**-0.5 * math.log2(math.e)
HIGH = 2.0**100
VMEM_MIB = 16


def contract_last(a, b):
    return lax.dot_general(a, b, (((1,), (1,)), ((), ())), preferred_element_type=jnp.float32)


def lane_sum(weights):
    parts = [weights[:, i : i + HEAD] for i in range(0, weights.shape[1], HEAD)]
    while len(parts) > 1:
        parts = [a + b for a, b in zip(parts[::2], parts[1::2])]
    return parts[0]


def own_masks(own_ref):
    ids = own_ref[2 * BLOCK :, :].astype(jnp.float32)
    key_ids = jnp.concatenate([ids[0:1, :], ids[1:2, :]], axis=1)
    key_ids = jnp.broadcast_to(key_ids, (BLOCK, BLOCK))
    query_ids = key_ids.T
    q_pos = lax.broadcasted_iota(jnp.int32, (BLOCK, BLOCK), 0)
    k_pos = lax.broadcasted_iota(jnp.int32, (BLOCK, BLOCK), 1)
    visible = (key_ids == query_ids) & (k_pos <= q_pos)
    in_first = (query_ids == key_ids[0:1, 0:1])[:, :HEAD]
    return visible, in_first


def add_own(q_ref, own_ref, shift_ref, l_ref, acc_ref):
    visible, in_first = own_masks(own_ref)
    keys = own_ref[:BLOCK, :]
    values = own_ref[BLOCK : 2 * BLOCK, :]
    for h in range(HEADS):
        rows = pl.ds(h * BLOCK, BLOCK)
        scores = contract_last(q_ref[:, h * HEAD : (h + 1) * HEAD], keys) * FACTOR
        scores = jnp.where(visible, scores, NEGATIVE)
        top = jnp.max(scores, axis=1, keepdims=True)
        weights = jnp.exp2(scores - top)
        l_ref[rows, :] = lane_sum(weights)
        acc_ref[rows, :] = jnp.dot(
            weights.astype(jnp.bfloat16), values, preferred_element_type=jnp.float32
        )
        shift_ref[rows, :] = jnp.where(
            in_first, jnp.broadcast_to(top, (BLOCK, HEAD)), -NEGATIVE
        )


def seen_rows(first_id, ids):
    ids = ids.astype(jnp.float32)
    return jnp.sum(jnp.where(ids == first_id, 1.0, 0.0)).astype(jnp.int32)


def gather(slots, counts, ok_ref, own_ref, k_buf, v_buf, part):
    first_id = own_ref[2 * BLOCK :, :].astype(jnp.float32)[0:1, 0:1]
    places = [(ref, k * SLOT) for ref, count in zip(slots, counts) for k in range(count)]
    seen = [seen_rows(first_id, ref[at + 2 * BLOCK : at + SLOT, :]) for ref, at in places]
    seen = [rows * ok_ref[i] for i, rows in enumerate(seen)]
    full = jnp.int32(0)
    partial = jnp.int32(0)
    for rows, (ref, at) in zip(seen, places):
        whole = rows == BLOCK

        @pl.when(whole)
        def _():
            to = pl.ds(pl.multiple_of(full * BLOCK, BLOCK), BLOCK)
            k_buf[to, :] = ref[at : at + BLOCK, :]
            v_buf[to, :] = ref[at + BLOCK : at + 2 * BLOCK, :]

        @pl.when((rows > 0) & (rows < BLOCK))
        def _():
            part[...] = ref[at : at + 2 * BLOCK, :]

        full = full + whole.astype(jnp.int32)
        partial = partial + jnp.where(whole, 0, rows)
    return full, partial


def add_blocks(full, partial, q_ref, shift_ref, l_ref, acc_ref, k_buf, v_buf, part):
    def attend(chunk, limit):
        at = pl.ds(pl.multiple_of(chunk * WIDE, WIDE), WIDE)
        keys, values = k_buf[at, :], v_buf[at, :]
        for h in range(0, HEADS, TOGETHER):
            rows = pl.ds(h * BLOCK, TOGETHER * BLOCK)
            some = [q_ref[:, i * HEAD : (i + 1) * HEAD] for i in range(h, h + TOGETHER)]
            scores = contract_last(jnp.concatenate(some, axis=0), keys) * FACTOR
            if limit is not None:
                scores = scores + limit
            shift = shift_ref[rows, :]
            weights = jnp.exp2(scores - jnp.concatenate([shift] * (WIDE // HEAD), axis=1))
            l_ref[rows, :] += lane_sum(weights)
            acc_ref[rows, :] += jnp.dot(
                weights.astype(jnp.bfloat16), values, preferred_element_type=jnp.float32
            )

    pairs = full // 2
    odd = full - 2 * pairs

    @pl.loop(0, pairs)
    def _(chunk):
        attend(chunk, None)

    @pl.when((odd > 0) | (partial > 0))
    def _():
        left = pl.ds(pl.multiple_of(pairs * WIDE, WIDE), BLOCK)
        right = pl.ds(pl.multiple_of(pairs * WIDE + BLOCK, BLOCK), BLOCK)
        none = jnp.zeros((BLOCK, HEAD), jnp.bfloat16)

        @pl.when(odd == 0)
        def _():
            k_buf[left, :] = none
            v_buf[left, :] = none

        @pl.when(partial > 0)
        def _():
            k_buf[right, :] = part[:BLOCK, :]
            v_buf[right, :] = part[BLOCK:, :]

        @pl.when(partial == 0)
        def _():
            k_buf[right, :] = none
            v_buf[right, :] = none

        k_pos = lax.broadcasted_iota(jnp.int32, (1, WIDE), 1)
        shown = ((k_pos < BLOCK) & (odd > 0)) | (k_pos >= WIDE - partial)
        attend(pairs, jnp.where(shown, 0.0, NEGATIVE))


def copies(pairs, sems):
    return [pltpu.make_async_copy(a, b, sems.at[i]) for i, (a, b) in enumerate(pairs)]


def run(moves):
    for move in moves:
        move.start()
    for move in moves:
        move.wait()


def own_kernel(q_hbm, own_ref, shift_out, l_out, acc_out, q, shift, l_sum, acc_sum, sems):
    fetch, *keep = copies(
        [(q_hbm, q), (shift, shift_out), (l_sum, l_out), (acc_sum, acc_out)], sems
    )
    fetch.start()
    fetch.wait()
    add_own(q, own_ref, shift, l_sum, acc_sum)
    run(keep)


def more_kernel(counts, *refs):
    n = len(counts)
    ok_ref, q_hbm, own_ref, shift_in, l_in, acc_in = refs[:6]
    slots = refs[6 : 6 + n]
    l_sum, acc_sum, q, shift, k_buf, v_buf, part, sems = refs[6 + n :]
    moves = copies([(q_hbm, q), (shift_in, shift), (l_in, l_sum), (acc_in, acc_sum)], sems)
    for move in moves:
        move.start()
    full, partial = gather(slots, counts, ok_ref, own_ref, k_buf, v_buf, part)
    for move in moves:
        move.wait()
    add_blocks(full, partial, q, shift, l_sum, acc_sum, k_buf, v_buf, part)


def last_kernel(counts, all_counts, *refs):
    n, m = len(counts), len(all_counts)
    ok_ref, all_ok_ref, q, own_ref, shift, l_in, acc_in = refs[:7]
    slots, everything = refs[7 : 7 + n], refs[7 + n : 7 + n + m]
    out_ref, l_sum, acc_sum, k_buf, v_buf, part, store, top, sems = refs[7 + n + m :]
    full, partial = gather(slots, counts, ok_ref, own_ref, k_buf, v_buf, part)
    l_sum[...] = l_in[...]
    acc_sum[...] = acc_in[...]
    add_blocks(full, partial, q, shift, l_sum, acc_sum, k_buf, v_buf, part)
    most = jnp.zeros((BLOCK, 1), jnp.float32)
    for h in range(HEADS):
        rows = pl.ds(h * BLOCK, BLOCK)
        total = jnp.sum(l_sum[rows, :], axis=1, keepdims=True)
        most = jnp.where(total <= HIGH, most, 1.0)
        out_ref[:, h * HEAD : (h + 1) * HEAD] = (acc_sum[rows, :] * (1.0 / total)).astype(
            jnp.bfloat16
        )

    @pl.when(jnp.max(most) > 0.5)
    def _():
        at = 0
        for ref, count in zip(everything, all_counts):
            for k in range(count):
                run(copies([(ref.at[k * SLOT : (k + 1) * SLOT, :], store.at[at])], sems))
                at += 1
        with_maximum(at, all_ok_ref, q, own_ref, store, top, l_sum, acc_sum, out_ref)


def with_maximum(count, ok_ref, q_ref, own_ref, store, top, l_sum, acc_sum, out_ref):
    visible, in_first = own_masks(own_ref)
    first_id = own_ref[2 * BLOCK :, :].astype(jnp.float32)[0:1, 0:1]
    own_bias = jnp.where(visible, 0.0, NEGATIVE)

    def head(h, carry):
        q = q_ref[:, pl.ds(pl.multiple_of(h * HEAD, HEAD), HEAD)]
        scores = contract_last(q, own_ref[:BLOCK, :]) * FACTOR + own_bias
        first_top = jnp.max(scores, axis=1, keepdims=True)
        weights = jnp.exp2(scores - first_top)
        top[...] = jnp.where(in_first, jnp.broadcast_to(first_top, (BLOCK, HEAD)), -NEGATIVE)
        l_sum[:BLOCK, :] = lane_sum(weights)
        acc_sum[:BLOCK, :] = jnp.dot(
            weights.astype(jnp.bfloat16),
            own_ref[BLOCK : 2 * BLOCK, :],
            preferred_element_type=jnp.float32,
        )

        def block(j, carry):
            seen = seen_rows(first_id, store[j, 2 * BLOCK :, :]) * ok_ref[j]

            @pl.when(seen > 0)
            def _():
                k_pos = lax.broadcasted_iota(jnp.int32, (1, BLOCK), 1)
                limit = jnp.where(k_pos >= BLOCK - seen, 0.0, NEGATIVE)
                scores = contract_last(q, store[j, :BLOCK, :]) * FACTOR + limit
                old = top[...]
                new = jnp.maximum(old, jnp.max(scores, axis=1, keepdims=True))
                fade = jnp.exp2(old - new)
                weights = jnp.exp2(scores - new[:, 0:1])
                l_sum[:BLOCK, :] = l_sum[:BLOCK, :] * fade + lane_sum(weights)
                acc_sum[:BLOCK, :] = acc_sum[:BLOCK, :] * fade + jnp.dot(
                    weights.astype(jnp.bfloat16),
                    store[j, BLOCK : 2 * BLOCK, :],
                    preferred_element_type=jnp.float32,
                )
                top[...] = new

            return carry

        lax.fori_loop(0, count, block, 0)
        total = jnp.sum(l_sum[:BLOCK, :], axis=1, keepdims=True)
        out_ref[:, pl.ds(pl.multiple_of(h * HEAD, HEAD), HEAD)] = (
            acc_sum[:BLOCK, :] * (1.0 / total)
        ).astype(jnp.bfloat16)
        return carry

    lax.fori_loop(0, HEADS, head, 0)


VMEM = pl.BlockSpec(memory_space=pltpu.VMEM)
SMEM = pl.BlockSpec(memory_space=pltpu.SMEM)
HBM = pl.BlockSpec(memory_space=pltpu.HBM)
SUMS = jax.ShapeDtypeStruct((HEADS * BLOCK, HEAD), jnp.float32)
COST = pl.CostEstimate(flops=1, bytes_accessed=1, transcendentals=0)


def params(mib):
    return pltpu.CompilerParams(vmem_limit_bytes=mib * 1024 * 1024)


def buffers(blocks):
    rows = (blocks + blocks % 2 + 2) * BLOCK
    return [
        pltpu.VMEM((rows, HEAD), jnp.bfloat16),
        pltpu.VMEM((rows, HEAD), jnp.bfloat16),
        pltpu.VMEM((2 * BLOCK, HEAD), jnp.bfloat16),
    ]


QUERIES = pltpu.VMEM((BLOCK, HEADS * HEAD), jnp.bfloat16)
SUM = pltpu.VMEM(SUMS.shape, jnp.float32)
SEMS = pltpu.SemaphoreType.DMA((4,))


def in_hbm(*arrays):
    return [pltpu.with_memory_space_constraint(a, pltpu.HBM) for a in arrays]


def stack_ok(ok):
    return jnp.stack([jnp.asarray(o, jnp.int32) for o in ok])


def attend_own(q, own):
    return pl.pallas_call(
        own_kernel,
        out_shape=[pltpu.HBM(SUMS.shape, SUMS.dtype)] * 3,
        in_specs=[HBM, VMEM],
        out_specs=[HBM] * 3,
        scratch_shapes=[QUERIES] + [SUM] * 3 + [SEMS],
        compiler_params=params(VMEM_MIB), cost_estimate=COST, name="attend_own",
    )(*in_hbm(q), own)


def attend_more(state, q, own, arrays, ok):
    counts = [a.shape[0] // SLOT for a in arrays]
    sums = pl.pallas_call(
        functools.partial(more_kernel, counts),
        out_shape=[SUMS] * 2,
        in_specs=[SMEM, HBM, VMEM] + [HBM] * 3 + [VMEM] * len(arrays),
        out_specs=[VMEM] * 2,
        scratch_shapes=[QUERIES, SUM] + buffers(sum(counts)) + [SEMS],
        compiler_params=params(VMEM_MIB), cost_estimate=COST, name="attend_more",
    )(stack_ok(ok), *in_hbm(q), own, *in_hbm(*state), *arrays)
    return state[0], *sums


def attend_last(state, q, own, arrays, ok, everything, all_ok):
    counts = [a.shape[0] // SLOT for a in arrays]
    all_counts = [a.shape[0] // SLOT for a in everything]
    return pl.pallas_call(
        functools.partial(last_kernel, counts, all_counts),
        out_shape=jax.ShapeDtypeStruct((BLOCK, HEADS * HEAD), jnp.bfloat16),
        in_specs=[SMEM] * 2 + [VMEM] * 5 + [VMEM] * len(arrays)
        + [pl.BlockSpec(memory_space=pl.ANY)] * len(everything),
        out_specs=VMEM,
        scratch_shapes=[SUM] * 2 + buffers(sum(counts))
        + [
            pltpu.VMEM((sum(all_counts), SLOT, HEAD), jnp.bfloat16),
            pltpu.VMEM((BLOCK, HEAD), jnp.float32),
            SEMS,
        ],
        compiler_params=params(VMEM_MIB), cost_estimate=COST, name="attend_last",
    )(stack_ok(ok), stack_ok(all_ok), q, own, *state, *arrays, *everything)


def exchange(v, mask):
    return lax.ppermute(v, "ctx", [(i, i ^ mask) for i in range(NX * NZ)])


def along_x(v, steps):
    return lax.ppermute(v, "ctx", [(i, i + NZ * steps) for i in range((NX - steps) * NZ)])


def together(*arrays):
    return lax.optimization_barrier(arrays)


def per_device(queries, keys, values, doc_ids):
    z = lax.axis_index("ctx") % NZ
    bit = [(z >> b) & 1 for b in range(3)]
    one = jnp.int32(1)
    ids = (doc_ids + 1).astype(jnp.bfloat16).reshape(2, HEAD)
    ids = jnp.pad(ids, ((0, IDS - 2), (0, 0)))
    (own,) = together(jnp.concatenate([keys, values, ids], axis=0))
    q = queries

    b0 = along_x(own, 1)
    c0 = along_x(own, 2)
    p2 = exchange(own, 2)
    p4 = exchange(own, 4)
    state = attend_own(q, own)
    state, p4, p2, b0, c0 = together(state, p4, p2, b0, c0)

    near1 = exchange(jnp.concatenate([b0, jnp.where(bit[0] == 0, own, c0)]), 1)
    pair = jnp.concatenate([p2, p4])
    p6 = exchange(p4, 2)
    b24 = along_x(pair, 1)
    c24 = along_x(pair, 2)
    (p6,) = together(p6)

    b6 = along_x(p6, 1)
    c6 = along_x(p6, 2)
    b24, c24 = together(b24, c24)

    sent = [
        b24,
        jnp.where(bit[1] == 1, p2, c24[:SLOT]),
        jnp.where(bit[2] == 1, p4, c24[SLOT:]),
    ]
    sent = jnp.concatenate(sent)
    near35 = exchange(sent, 1)
    b6, c6, sent = together(b6, c6, sent)

    near7 = exchange(jnp.concatenate([b6, jnp.where(bit[2] == 1, p6, c6)]), 1)
    state = attend_more(
        state,
        q,
        own,
        [p4, p2, b0, c0, near1, b24, c24, p6, b6, c6],
        [bit[2], bit[1]] + [one] * 8 + [bit[2]] + [one] * 2,
    )
    arrays = [p2, p4, b0, c0, near1, b24, c24, p6, near35, b6, c6, near7]
    ok = [bit[1], bit[2]] + [one] * 8 + [bit[2]] + [one] * 8
    return attend_last(state, q, own, [near35, near7], [one] * 6, arrays, ok)


def solution(mesh):
    return jax.shard_map(
        per_device,
        mesh=mesh,
        in_specs=(
            P(("dp", "ctx"), "tp"),
            P(("dp", "ctx"), "tp"),
            P(("dp", "ctx"), "tp"),
            P(("dp", "ctx")),
        ),
        out_specs=P(("dp", "ctx"), "tp"),
        check_vma=False,
    )
```

```python
import functools
import math

import jax
import jax.numpy as jnp
from jax import lax
from jax.experimental import pallas as pl
from jax.experimental.pallas import tpu as pltpu
from jax.sharding import PartitionSpec as P

HEAD = 128
BLOCK = 256
HEADS = 8
TOGETHER = 4
IDS = 16
SLOT = 2 * BLOCK + IDS
WIDE = 2 * BLOCK
NX, NZ = 4, 8
NEGATIVE = -1e30
FACTOR = HEAD**-0.5 * math.log2(math.e)
HIGH = 2.0**100
VMEM_MIB = 16


def contract_last(a, b):
    return lax.dot_general(a, b, (((1,), (1,)), ((), ())), preferred_element_type=jnp.float32)


def lane_sum(weights):
    parts = [weights[:, i : i + HEAD] for i in range(0, weights.shape[1], HEAD)]
    while len(parts) > 1:
        parts = [a + b for a, b in zip(parts[::2], parts[1::2])]
    return parts[0]


def own_masks(own_ref):
    ids = own_ref[2 * BLOCK :, :].astype(jnp.float32)
    key_ids = jnp.concatenate([ids[0:1, :], ids[1:2, :]], axis=1)
    key_ids = jnp.broadcast_to(key_ids, (BLOCK, BLOCK))
    query_ids = key_ids.T
    q_pos = lax.broadcasted_iota(jnp.int32, (BLOCK, BLOCK), 0)
    k_pos = lax.broadcasted_iota(jnp.int32, (BLOCK, BLOCK), 1)
    visible = (key_ids == query_ids) & (k_pos <= q_pos)
    in_first = (query_ids == key_ids[0:1, 0:1])[:, :HEAD]
    return visible, in_first


def add_own(q_ref, own_ref, shift_ref, l_ref, acc_ref):
    visible, in_first = own_masks(own_ref)
    keys = own_ref[:BLOCK, :]
    values = own_ref[BLOCK : 2 * BLOCK, :]
    for h in range(HEADS):
        rows = pl.ds(h * BLOCK, BLOCK)
        scores = contract_last(q_ref[:, h * HEAD : (h + 1) * HEAD], keys) * FACTOR
        scores = jnp.where(visible, scores, NEGATIVE)
        top = jnp.max(scores, axis=1, keepdims=True)
        weights = jnp.exp2(scores - top)
        l_ref[rows, :] = lane_sum(weights)
        acc_ref[rows, :] = jnp.dot(
            weights.astype(jnp.bfloat16), values, preferred_element_type=jnp.float32
        )
        shift_ref[rows, :] = jnp.where(
            in_first, jnp.broadcast_to(top, (BLOCK, HEAD)), -NEGATIVE
        )


def seen_rows(first_id, ids):
    ids = ids.astype(jnp.float32)
    return jnp.sum(jnp.where(ids == first_id, 1.0, 0.0)).astype(jnp.int32)


def gather(slots, counts, ok_ref, own_ref, k_buf, v_buf, part):
    first_id = own_ref[2 * BLOCK :, :].astype(jnp.float32)[0:1, 0:1]
    places = [(ref, k * SLOT) for ref, count in zip(slots, counts) for k in range(count)]
    seen = [seen_rows(first_id, ref[at + 2 * BLOCK : at + SLOT, :]) for ref, at in places]
    seen = [rows * ok_ref[i] for i, rows in enumerate(seen)]
    full = jnp.int32(0)
    partial = jnp.int32(0)
    for rows, (ref, at) in zip(seen, places):
        whole = rows == BLOCK

        @pl.when(whole)
        def _():
            to = pl.ds(pl.multiple_of(full * BLOCK, BLOCK), BLOCK)
            k_buf[to, :] = ref[at : at + BLOCK, :]
            v_buf[to, :] = ref[at + BLOCK : at + 2 * BLOCK, :]

        @pl.when((rows > 0) & (rows < BLOCK))
        def _():
            part[...] = ref[at : at + 2 * BLOCK, :]

        full = full + whole.astype(jnp.int32)
        partial = partial + jnp.where(whole, 0, rows)
    return full, partial


def add_blocks(full, partial, q_ref, shift_ref, l_ref, acc_ref, k_buf, v_buf, part):
    def attend(chunk, limit):
        at = pl.ds(pl.multiple_of(chunk * WIDE, WIDE), WIDE)
        keys, values = k_buf[at, :], v_buf[at, :]
        for h in range(0, HEADS, TOGETHER):
            rows = pl.ds(h * BLOCK, TOGETHER * BLOCK)
            some = [q_ref[:, i * HEAD : (i + 1) * HEAD] for i in range(h, h + TOGETHER)]
            scores = contract_last(jnp.concatenate(some, axis=0), keys) * FACTOR
            if limit is not None:
                scores = scores + limit
            shift = shift_ref[rows, :]
            weights = jnp.exp2(scores - jnp.concatenate([shift] * (WIDE // HEAD), axis=1))
            l_ref[rows, :] += lane_sum(weights)
            acc_ref[rows, :] += jnp.dot(
                weights.astype(jnp.bfloat16), values, preferred_element_type=jnp.float32
            )

    pairs = full // 2
    odd = full - 2 * pairs

    @pl.loop(0, pairs)
    def _(chunk):
        attend(chunk, None)

    @pl.when((odd > 0) | (partial > 0))
    def _():
        left = pl.ds(pl.multiple_of(pairs * WIDE, WIDE), BLOCK)
        right = pl.ds(pl.multiple_of(pairs * WIDE + BLOCK, BLOCK), BLOCK)
        none = jnp.zeros((BLOCK, HEAD), jnp.bfloat16)

        @pl.when(odd == 0)
        def _():
            k_buf[left, :] = none
            v_buf[left, :] = none

        @pl.when(partial > 0)
        def _():
            k_buf[right, :] = part[:BLOCK, :]
            v_buf[right, :] = part[BLOCK:, :]

        @pl.when(partial == 0)
        def _():
            k_buf[right, :] = none
            v_buf[right, :] = none

        k_pos = lax.broadcasted_iota(jnp.int32, (1, WIDE), 1)
        shown = ((k_pos < BLOCK) & (odd > 0)) | (k_pos >= WIDE - partial)
        attend(pairs, jnp.where(shown, 0.0, NEGATIVE))


def copies(pairs, sems):
    return [pltpu.make_async_copy(a, b, sems.at[i]) for i, (a, b) in enumerate(pairs)]


def run(moves):
    for move in moves:
        move.start()
    for move in moves:
        move.wait()


def own_kernel(q_hbm, own_ref, shift_out, l_out, acc_out, q, shift, l_sum, acc_sum, sems):
    fetch, *keep = copies(
        [(q_hbm, q), (shift, shift_out), (l_sum, l_out), (acc_sum, acc_out)], sems
    )
    fetch.start()
    fetch.wait()
    add_own(q, own_ref, shift, l_sum, acc_sum)
    run(keep)


def more_kernel(counts, *refs):
    n = len(counts)
    ok_ref, q_hbm, own_ref, shift_in, l_in, acc_in = refs[:6]
    slots = refs[6 : 6 + n]
    l_sum, acc_sum, q, shift, k_buf, v_buf, part, sems = refs[6 + n :]
    moves = copies([(q_hbm, q), (shift_in, shift), (l_in, l_sum), (acc_in, acc_sum)], sems)
    for move in moves:
        move.start()
    full, partial = gather(slots, counts, ok_ref, own_ref, k_buf, v_buf, part)
    for move in moves:
        move.wait()
    add_blocks(full, partial, q, shift, l_sum, acc_sum, k_buf, v_buf, part)


def last_kernel(counts, all_counts, *refs):
    n, m = len(counts), len(all_counts)
    ok_ref, all_ok_ref, q, own_ref, shift, l_in, acc_in = refs[:7]
    slots, everything = refs[7 : 7 + n], refs[7 + n : 7 + n + m]
    out_ref, l_sum, acc_sum, k_buf, v_buf, part, store, top, sems = refs[7 + n + m :]
    full, partial = gather(slots, counts, ok_ref, own_ref, k_buf, v_buf, part)
    l_sum[...] = l_in[...]
    acc_sum[...] = acc_in[...]
    add_blocks(full, partial, q, shift, l_sum, acc_sum, k_buf, v_buf, part)
    most = jnp.zeros((BLOCK, 1), jnp.float32)
    for h in range(HEADS):
        rows = pl.ds(h * BLOCK, BLOCK)
        total = jnp.sum(l_sum[rows, :], axis=1, keepdims=True)
        most = jnp.where(total <= HIGH, most, 1.0)
        out_ref[:, h * HEAD : (h + 1) * HEAD] = (acc_sum[rows, :] * (1.0 / total)).astype(
            jnp.bfloat16
        )

    @pl.when(jnp.max(most) > 0.5)
    def _():
        at = 0
        for ref, count in zip(everything, all_counts):
            for k in range(count):
                run(copies([(ref.at[k * SLOT : (k + 1) * SLOT, :], store.at[at])], sems))
                at += 1
        with_maximum(at, all_ok_ref, q, own_ref, store, top, l_sum, acc_sum, out_ref)


def with_maximum(count, ok_ref, q_ref, own_ref, store, top, l_sum, acc_sum, out_ref):
    visible, in_first = own_masks(own_ref)
    first_id = own_ref[2 * BLOCK :, :].astype(jnp.float32)[0:1, 0:1]
    own_bias = jnp.where(visible, 0.0, NEGATIVE)

    def head(h, carry):
        q = q_ref[:, pl.ds(pl.multiple_of(h * HEAD, HEAD), HEAD)]
        scores = contract_last(q, own_ref[:BLOCK, :]) * FACTOR + own_bias
        first_top = jnp.max(scores, axis=1, keepdims=True)
        weights = jnp.exp2(scores - first_top)
        top[...] = jnp.where(in_first, jnp.broadcast_to(first_top, (BLOCK, HEAD)), -NEGATIVE)
        l_sum[:BLOCK, :] = lane_sum(weights)
        acc_sum[:BLOCK, :] = jnp.dot(
            weights.astype(jnp.bfloat16),
            own_ref[BLOCK : 2 * BLOCK, :],
            preferred_element_type=jnp.float32,
        )

        def block(j, carry):
            seen = seen_rows(first_id, store[j, 2 * BLOCK :, :]) * ok_ref[j]

            @pl.when(seen > 0)
            def _():
                k_pos = lax.broadcasted_iota(jnp.int32, (1, BLOCK), 1)
                limit = jnp.where(k_pos >= BLOCK - seen, 0.0, NEGATIVE)
                scores = contract_last(q, store[j, :BLOCK, :]) * FACTOR + limit
                old = top[...]
                new = jnp.maximum(old, jnp.max(scores, axis=1, keepdims=True))
                fade = jnp.exp2(old - new)
                weights = jnp.exp2(scores - new[:, 0:1])
                l_sum[:BLOCK, :] = l_sum[:BLOCK, :] * fade + lane_sum(weights)
                acc_sum[:BLOCK, :] = acc_sum[:BLOCK, :] * fade + jnp.dot(
                    weights.astype(jnp.bfloat16),
                    store[j, BLOCK : 2 * BLOCK, :],
                    preferred_element_type=jnp.float32,
                )
                top[...] = new

            return carry

        lax.fori_loop(0, count, block, 0)
        total = jnp.sum(l_sum[:BLOCK, :], axis=1, keepdims=True)
        out_ref[:, pl.ds(pl.multiple_of(h * HEAD, HEAD), HEAD)] = (
            acc_sum[:BLOCK, :] * (1.0 / total)
        ).astype(jnp.bfloat16)
        return carry

    lax.fori_loop(0, HEADS, head, 0)


VMEM = pl.BlockSpec(memory_space=pltpu.VMEM)
SMEM = pl.BlockSpec(memory_space=pltpu.SMEM)
HBM = pl.BlockSpec(memory_space=pltpu.HBM)
SUMS = jax.ShapeDtypeStruct((HEADS * BLOCK, HEAD), jnp.float32)
COST = pl.CostEstimate(flops=1, bytes_accessed=1, transcendentals=0)


def params(mib):
    return pltpu.CompilerParams(vmem_limit_bytes=mib * 1024 * 1024)


def buffers(blocks):
    rows = (blocks + blocks % 2 + 2) * BLOCK
    return [
        pltpu.VMEM((rows, HEAD), jnp.bfloat16),
        pltpu.VMEM((rows, HEAD), jnp.bfloat16),
        pltpu.VMEM((2 * BLOCK, HEAD), jnp.bfloat16),
    ]


QUERIES = pltpu.VMEM((BLOCK, HEADS * HEAD), jnp.bfloat16)
SUM = pltpu.VMEM(SUMS.shape, jnp.float32)
SEMS = pltpu.SemaphoreType.DMA((4,))


def in_hbm(*arrays):
    return [pltpu.with_memory_space_constraint(a, pltpu.HBM) for a in arrays]


def stack_ok(ok):
    return jnp.stack([jnp.asarray(o, jnp.int32) for o in ok])


def attend_own(q, own):
    return pl.pallas_call(
        own_kernel,
        out_shape=[pltpu.HBM(SUMS.shape, SUMS.dtype)] * 3,
        in_specs=[HBM, VMEM],
        out_specs=[HBM] * 3,
        scratch_shapes=[QUERIES] + [SUM] * 3 + [SEMS],
        compiler_params=params(VMEM_MIB), cost_estimate=COST, name="attend_own",
    )(*in_hbm(q), own)


def attend_more(state, q, own, arrays, ok):
    counts = [a.shape[0] // SLOT for a in arrays]
    sums = pl.pallas_call(
        functools.partial(more_kernel, counts),
        out_shape=[SUMS] * 2,
        in_specs=[SMEM, HBM, VMEM] + [HBM] * 3 + [VMEM] * len(arrays),
        out_specs=[VMEM] * 2,
        scratch_shapes=[QUERIES, SUM] + buffers(sum(counts)) + [SEMS],
        compiler_params=params(VMEM_MIB), cost_estimate=COST, name="attend_more",
    )(stack_ok(ok), *in_hbm(q), own, *in_hbm(*state), *arrays)
    return state[0], *sums


def attend_last(state, q, own, arrays, ok, everything, all_ok):
    counts = [a.shape[0] // SLOT for a in arrays]
    all_counts = [a.shape[0] // SLOT for a in everything]
    return pl.pallas_call(
        functools.partial(last_kernel, counts, all_counts),
        out_shape=jax.ShapeDtypeStruct((BLOCK, HEADS * HEAD), jnp.bfloat16),
        in_specs=[SMEM] * 2 + [VMEM] * 5 + [VMEM] * len(arrays)
        + [pl.BlockSpec(memory_space=pl.ANY)] * len(everything),
        out_specs=VMEM,
        scratch_shapes=[SUM] * 2 + buffers(sum(counts))
        + [
            pltpu.VMEM((sum(all_counts), SLOT, HEAD), jnp.bfloat16),
            pltpu.VMEM((BLOCK, HEAD), jnp.float32),
            SEMS,
        ],
        compiler_params=params(VMEM_MIB), cost_estimate=COST, name="attend_last",
    )(stack_ok(ok), stack_ok(all_ok), q, own, *state, *arrays, *everything)


def exchange(v, mask):
    return lax.ppermute(v, "ctx", [(i, i ^ mask) for i in range(NX * NZ)])


def along_x(v, steps):
    return lax.ppermute(v, "ctx", [(i, i + NZ * steps) for i in range((NX - steps) * NZ)])


def together(*arrays):
    return lax.optimization_barrier(arrays)


def per_device(queries, keys, values, doc_ids):
    z = lax.axis_index("ctx") % NZ
    bit = [(z >> b) & 1 for b in range(3)]
    one = jnp.int32(1)
    ids = (doc_ids + 1).astype(jnp.bfloat16).reshape(2, HEAD)
    ids = jnp.pad(ids, ((0, IDS - 2), (0, 0)))
    (own,) = together(jnp.concatenate([keys, values, ids], axis=0))
    q = queries

    b0 = along_x(own, 1)
    c0 = along_x(own, 2)
    p2 = exchange(own, 2)
    p4 = exchange(own, 4)
    state = attend_own(q, own)
    state, p4, p2, b0, c0 = together(state, p4, p2, b0, c0)

    near1 = exchange(jnp.concatenate([b0, jnp.where(bit[0] == 0, own, c0)]), 1)
    pair = jnp.concatenate([p2, p4])
    p6 = exchange(p4, 2)
    b24 = along_x(pair, 1)
    c24 = along_x(pair, 2)
    state, p6 = together(state, p6)

    b6 = along_x(p6, 1)
    c6 = along_x(p6, 2)
    b24, c24 = together(b24, c24)

    sent = [
        b24,
        jnp.where(bit[1] == 1, p2, c24[:SLOT]),
        jnp.where(bit[2] == 1, p4, c24[SLOT:]),
    ]
    sent = jnp.concatenate(sent)
    near35 = exchange(sent, 1)
    b6, c6, sent = together(b6, c6, sent)

    near7 = exchange(jnp.concatenate([b6, jnp.where(bit[2] == 1, p6, c6)]), 1)
    state = attend_more(
        state,
        q,
        own,
        [p4, p2, b0, c0, near1, b24, c24, p6, b6, c6],
        [bit[2], bit[1]] + [one] * 8 + [bit[2]] + [one] * 2,
    )
    arrays = [p2, p4, b0, c0, near1, b24, c24, p6, near35, b6, c6, near7]
    ok = [bit[1], bit[2]] + [one] * 8 + [bit[2]] + [one] * 8
    return attend_last(state, q, own, [near35, near7], [one] * 6, arrays, ok)


def solution(mesh):
    return jax.shard_map(
        per_device,
        mesh=mesh,
        in_specs=(
            P(("dp", "ctx"), "tp"),
            P(("dp", "ctx"), "tp"),
            P(("dp", "ctx"), "tp"),
            P(("dp", "ctx")),
        ),
        out_specs=P(("dp", "ctx"), "tp"),
        check_vma=False,
    )
```

```python
import functools
import math

import jax
import jax.numpy as jnp
from jax import lax
from jax.experimental import pallas as pl
from jax.experimental.pallas import tpu as pltpu
from jax.sharding import PartitionSpec as P

HEAD = 128
BLOCK = 256
HEADS = 8
TOGETHER = 4
IDS = 16
SLOT = 2 * BLOCK + IDS
WIDE = 2 * BLOCK
NX, NZ = 4, 8
NEGATIVE = -1e30
FACTOR = HEAD**-0.5 * math.log2(math.e)
HIGH = 2.0**100
VMEM_MIB = 16


def contract_last(a, b):
    return lax.dot_general(a, b, (((1,), (1,)), ((), ())), preferred_element_type=jnp.float32)


def lane_sum(weights):
    parts = [weights[:, i : i + HEAD] for i in range(0, weights.shape[1], HEAD)]
    while len(parts) > 1:
        parts = [a + b for a, b in zip(parts[::2], parts[1::2])]
    return parts[0]


def own_masks(own_ref):
    ids = own_ref[2 * BLOCK :, :].astype(jnp.float32)
    key_ids = jnp.concatenate([ids[0:1, :], ids[1:2, :]], axis=1)
    key_ids = jnp.broadcast_to(key_ids, (BLOCK, BLOCK))
    query_ids = key_ids.T
    q_pos = lax.broadcasted_iota(jnp.int32, (BLOCK, BLOCK), 0)
    k_pos = lax.broadcasted_iota(jnp.int32, (BLOCK, BLOCK), 1)
    visible = (key_ids == query_ids) & (k_pos <= q_pos)
    in_first = (query_ids == key_ids[0:1, 0:1])[:, :HEAD]
    return visible, in_first


def add_own(q_ref, own_ref, shift_ref, l_ref, acc_ref, send):
    visible, in_first = own_masks(own_ref)
    keys = own_ref[:BLOCK, :]
    values = own_ref[BLOCK : 2 * BLOCK, :]
    for h in range(HEADS):
        rows = pl.ds(h * BLOCK, BLOCK)
        scores = contract_last(q_ref[:, h * HEAD : (h + 1) * HEAD], keys) * FACTOR
        scores = jnp.where(visible, scores, NEGATIVE)
        top = jnp.max(scores, axis=1, keepdims=True)
        weights = jnp.exp2(scores - top)
        l_ref[rows, :] = lane_sum(weights)
        acc_ref[rows, :] = jnp.dot(
            weights.astype(jnp.bfloat16), values, preferred_element_type=jnp.float32
        )
        shift_ref[rows, :] = jnp.where(
            in_first, jnp.broadcast_to(top, (BLOCK, HEAD)), -NEGATIVE
        )
        send(h)


def seen_rows(first_id, ids):
    ids = ids.astype(jnp.float32)
    return jnp.sum(jnp.where(ids == first_id, 1.0, 0.0)).astype(jnp.int32)


def gather(slots, counts, ok_ref, own_ref, k_buf, v_buf, part):
    first_id = own_ref[2 * BLOCK :, :].astype(jnp.float32)[0:1, 0:1]
    places = [(ref, k * SLOT) for ref, count in zip(slots, counts) for k in range(count)]
    seen = [seen_rows(first_id, ref[at + 2 * BLOCK : at + SLOT, :]) for ref, at in places]
    seen = [rows * ok_ref[i] for i, rows in enumerate(seen)]
    full = jnp.int32(0)
    partial = jnp.int32(0)
    for rows, (ref, at) in zip(seen, places):
        whole = rows == BLOCK

        @pl.when(whole)
        def _():
            to = pl.ds(pl.multiple_of(full * BLOCK, BLOCK), BLOCK)
            k_buf[to, :] = ref[at : at + BLOCK, :]
            v_buf[to, :] = ref[at + BLOCK : at + 2 * BLOCK, :]

        @pl.when((rows > 0) & (rows < BLOCK))
        def _():
            part[...] = ref[at : at + 2 * BLOCK, :]

        full = full + whole.astype(jnp.int32)
        partial = partial + jnp.where(whole, 0, rows)
    return full, partial


def add_blocks(full, partial, q_ref, shift_ref, l_ref, acc_ref, k_buf, v_buf, part):
    def attend(chunk, limit):
        at = pl.ds(pl.multiple_of(chunk * WIDE, WIDE), WIDE)
        keys, values = k_buf[at, :], v_buf[at, :]
        for h in range(0, HEADS, TOGETHER):
            rows = pl.ds(h * BLOCK, TOGETHER * BLOCK)
            some = [q_ref[:, i * HEAD : (i + 1) * HEAD] for i in range(h, h + TOGETHER)]
            scores = contract_last(jnp.concatenate(some, axis=0), keys) * FACTOR
            if limit is not None:
                scores = scores + limit
            shift = shift_ref[rows, :]
            weights = jnp.exp2(scores - jnp.concatenate([shift] * (WIDE // HEAD), axis=1))
            l_ref[rows, :] += lane_sum(weights)
            acc_ref[rows, :] += jnp.dot(
                weights.astype(jnp.bfloat16), values, preferred_element_type=jnp.float32
            )

    pairs = full // 2
    odd = full - 2 * pairs

    @pl.loop(0, pairs)
    def _(chunk):
        attend(chunk, None)

    @pl.when((odd > 0) | (partial > 0))
    def _():
        left = pl.ds(pl.multiple_of(pairs * WIDE, WIDE), BLOCK)
        right = pl.ds(pl.multiple_of(pairs * WIDE + BLOCK, BLOCK), BLOCK)
        none = jnp.zeros((BLOCK, HEAD), jnp.bfloat16)

        @pl.when(odd == 0)
        def _():
            k_buf[left, :] = none
            v_buf[left, :] = none

        @pl.when(partial > 0)
        def _():
            k_buf[right, :] = part[:BLOCK, :]
            v_buf[right, :] = part[BLOCK:, :]

        @pl.when(partial == 0)
        def _():
            k_buf[right, :] = none
            v_buf[right, :] = none

        k_pos = lax.broadcasted_iota(jnp.int32, (1, WIDE), 1)
        shown = ((k_pos < BLOCK) & (odd > 0)) | (k_pos >= WIDE - partial)
        attend(pairs, jnp.where(shown, 0.0, NEGATIVE))


def copies(pairs, sems):
    return [pltpu.make_async_copy(a, b, sems.at[i]) for i, (a, b) in enumerate(pairs)]


def run(moves):
    for move in moves:
        move.start()
    for move in moves:
        move.wait()


def own_kernel(q_hbm, own_ref, shift_out, l_out, acc_out, q, shift, l_sum, acc_sum, sems):
    fetch = copies([(q_hbm, q)], sems)
    run(fetch)
    pairs = [(shift, shift_out), (l_sum, l_out), (acc_sum, acc_out)]
    keep = []

    def send(h):
        rows = pl.ds(h * BLOCK, BLOCK)
        for i, (a, b) in enumerate(pairs):
            sem = sems.at[1 + 3 * h + i]
            keep.append(pltpu.make_async_copy(a.at[rows, :], b.at[rows, :], sem))
            keep[-1].start()

    add_own(q, own_ref, shift, l_sum, acc_sum, send)
    for move in keep:
        move.wait()


def more_kernel(counts, *refs):
    n = len(counts)
    ok_ref, q_hbm, own_ref, shift_in, l_in, acc_in = refs[:6]
    slots = refs[6 : 6 + n]
    l_sum, acc_sum, q, shift, k_buf, v_buf, part, sems = refs[6 + n :]
    moves = copies([(q_hbm, q), (shift_in, shift), (l_in, l_sum), (acc_in, acc_sum)], sems)
    for move in moves:
        move.start()
    full, partial = gather(slots, counts, ok_ref, own_ref, k_buf, v_buf, part)
    for move in moves:
        move.wait()
    add_blocks(full, partial, q, shift, l_sum, acc_sum, k_buf, v_buf, part)


def last_kernel(counts, all_counts, *refs):
    n, m = len(counts), len(all_counts)
    ok_ref, all_ok_ref, q, own_ref, shift, l_in, acc_in = refs[:7]
    slots, everything = refs[7 : 7 + n], refs[7 + n : 7 + n + m]
    out_ref, l_sum, acc_sum, k_buf, v_buf, part, store, top, sems = refs[7 + n + m :]
    full, partial = gather(slots, counts, ok_ref, own_ref, k_buf, v_buf, part)
    l_sum[...] = l_in[...]
    acc_sum[...] = acc_in[...]
    add_blocks(full, partial, q, shift, l_sum, acc_sum, k_buf, v_buf, part)
    most = jnp.zeros((BLOCK, 1), jnp.float32)
    for h in range(HEADS):
        rows = pl.ds(h * BLOCK, BLOCK)
        total = jnp.sum(l_sum[rows, :], axis=1, keepdims=True)
        most = jnp.where(total <= HIGH, most, 1.0)
        out_ref[:, h * HEAD : (h + 1) * HEAD] = (acc_sum[rows, :] * (1.0 / total)).astype(
            jnp.bfloat16
        )

    @pl.when(jnp.max(most) > 0.5)
    def _():
        at = 0
        for ref, count in zip(everything, all_counts):
            for k in range(count):
                run(copies([(ref.at[k * SLOT : (k + 1) * SLOT, :], store.at[at])], sems))
                at += 1
        with_maximum(at, all_ok_ref, q, own_ref, store, top, l_sum, acc_sum, out_ref)


def with_maximum(count, ok_ref, q_ref, own_ref, store, top, l_sum, acc_sum, out_ref):
    visible, in_first = own_masks(own_ref)
    first_id = own_ref[2 * BLOCK :, :].astype(jnp.float32)[0:1, 0:1]
    own_bias = jnp.where(visible, 0.0, NEGATIVE)

    def head(h, carry):
        q = q_ref[:, pl.ds(pl.multiple_of(h * HEAD, HEAD), HEAD)]
        scores = contract_last(q, own_ref[:BLOCK, :]) * FACTOR + own_bias
        first_top = jnp.max(scores, axis=1, keepdims=True)
        weights = jnp.exp2(scores - first_top)
        top[...] = jnp.where(in_first, jnp.broadcast_to(first_top, (BLOCK, HEAD)), -NEGATIVE)
        l_sum[:BLOCK, :] = lane_sum(weights)
        acc_sum[:BLOCK, :] = jnp.dot(
            weights.astype(jnp.bfloat16),
            own_ref[BLOCK : 2 * BLOCK, :],
            preferred_element_type=jnp.float32,
        )

        def block(j, carry):
            seen = seen_rows(first_id, store[j, 2 * BLOCK :, :]) * ok_ref[j]

            @pl.when(seen > 0)
            def _():
                k_pos = lax.broadcasted_iota(jnp.int32, (1, BLOCK), 1)
                limit = jnp.where(k_pos >= BLOCK - seen, 0.0, NEGATIVE)
                scores = contract_last(q, store[j, :BLOCK, :]) * FACTOR + limit
                old = top[...]
                new = jnp.maximum(old, jnp.max(scores, axis=1, keepdims=True))
                fade = jnp.exp2(old - new)
                weights = jnp.exp2(scores - new[:, 0:1])
                l_sum[:BLOCK, :] = l_sum[:BLOCK, :] * fade + lane_sum(weights)
                acc_sum[:BLOCK, :] = acc_sum[:BLOCK, :] * fade + jnp.dot(
                    weights.astype(jnp.bfloat16),
                    store[j, BLOCK : 2 * BLOCK, :],
                    preferred_element_type=jnp.float32,
                )
                top[...] = new

            return carry

        lax.fori_loop(0, count, block, 0)
        total = jnp.sum(l_sum[:BLOCK, :], axis=1, keepdims=True)
        out_ref[:, pl.ds(pl.multiple_of(h * HEAD, HEAD), HEAD)] = (
            acc_sum[:BLOCK, :] * (1.0 / total)
        ).astype(jnp.bfloat16)
        return carry

    lax.fori_loop(0, HEADS, head, 0)


VMEM = pl.BlockSpec(memory_space=pltpu.VMEM)
SMEM = pl.BlockSpec(memory_space=pltpu.SMEM)
HBM = pl.BlockSpec(memory_space=pltpu.HBM)
SUMS = jax.ShapeDtypeStruct((HEADS * BLOCK, HEAD), jnp.float32)
COST = pl.CostEstimate(flops=1, bytes_accessed=1, transcendentals=0)


def params(mib):
    return pltpu.CompilerParams(vmem_limit_bytes=mib * 1024 * 1024)


def buffers(blocks):
    rows = (blocks + blocks % 2 + 2) * BLOCK
    return [
        pltpu.VMEM((rows, HEAD), jnp.bfloat16),
        pltpu.VMEM((rows, HEAD), jnp.bfloat16),
        pltpu.VMEM((2 * BLOCK, HEAD), jnp.bfloat16),
    ]


QUERIES = pltpu.VMEM((BLOCK, HEADS * HEAD), jnp.bfloat16)
SUM = pltpu.VMEM(SUMS.shape, jnp.float32)
SEMS = pltpu.SemaphoreType.DMA((4,))


def in_hbm(*arrays):
    return [pltpu.with_memory_space_constraint(a, pltpu.HBM) for a in arrays]


def stack_ok(ok):
    return jnp.stack([jnp.asarray(o, jnp.int32) for o in ok])


def attend_own(q, own):
    return pl.pallas_call(
        own_kernel,
        out_shape=[pltpu.HBM(SUMS.shape, SUMS.dtype)] * 3,
        in_specs=[HBM, VMEM],
        out_specs=[HBM] * 3,
        scratch_shapes=[QUERIES] + [SUM] * 3 + [pltpu.SemaphoreType.DMA((1 + 3 * HEADS,))],
        compiler_params=params(VMEM_MIB), cost_estimate=COST, name="attend_own",
    )(*in_hbm(q), own)


def attend_more(state, q, own, arrays, ok):
    counts = [a.shape[0] // SLOT for a in arrays]
    sums = pl.pallas_call(
        functools.partial(more_kernel, counts),
        out_shape=[SUMS] * 2,
        in_specs=[SMEM, HBM, VMEM] + [HBM] * 3 + [VMEM] * len(arrays),
        out_specs=[VMEM] * 2,
        scratch_shapes=[QUERIES, SUM] + buffers(sum(counts)) + [SEMS],
        compiler_params=params(VMEM_MIB), cost_estimate=COST, name="attend_more",
    )(stack_ok(ok), *in_hbm(q), own, *in_hbm(*state), *arrays)
    return state[0], *sums


def attend_last(state, q, own, arrays, ok, everything, all_ok):
    counts = [a.shape[0] // SLOT for a in arrays]
    all_counts = [a.shape[0] // SLOT for a in everything]
    return pl.pallas_call(
        functools.partial(last_kernel, counts, all_counts),
        out_shape=jax.ShapeDtypeStruct((BLOCK, HEADS * HEAD), jnp.bfloat16),
        in_specs=[SMEM] * 2 + [VMEM] * 5 + [VMEM] * len(arrays)
        + [pl.BlockSpec(memory_space=pl.ANY)] * len(everything),
        out_specs=VMEM,
        scratch_shapes=[SUM] * 2 + buffers(sum(counts))
        + [
            pltpu.VMEM((sum(all_counts), SLOT, HEAD), jnp.bfloat16),
            pltpu.VMEM((BLOCK, HEAD), jnp.float32),
            SEMS,
        ],
        compiler_params=params(VMEM_MIB), cost_estimate=COST, name="attend_last",
    )(stack_ok(ok), stack_ok(all_ok), q, own, *state, *arrays, *everything)


def exchange(v, mask):
    return lax.ppermute(v, "ctx", [(i, i ^ mask) for i in range(NX * NZ)])


def along_x(v, steps):
    return lax.ppermute(v, "ctx", [(i, i + NZ * steps) for i in range((NX - steps) * NZ)])


def together(*arrays):
    return lax.optimization_barrier(arrays)


def per_device(queries, keys, values, doc_ids):
    z = lax.axis_index("ctx") % NZ
    bit = [(z >> b) & 1 for b in range(3)]
    one = jnp.int32(1)
    ids = (doc_ids + 1).astype(jnp.bfloat16).reshape(2, HEAD)
    ids = jnp.pad(ids, ((0, IDS - 2), (0, 0)))
    (own,) = together(jnp.concatenate([keys, values, ids], axis=0))
    q = queries

    b0 = along_x(own, 1)
    c0 = along_x(own, 2)
    p2 = exchange(own, 2)
    p4 = exchange(own, 4)
    state = attend_own(q, own)
    state, p4, p2, b0, c0 = together(state, p4, p2, b0, c0)

    near1 = exchange(jnp.concatenate([b0, jnp.where(bit[0] == 0, own, c0)]), 1)
    pair = jnp.concatenate([p2, p4])
    p6 = exchange(p4, 2)
    b24 = along_x(pair, 1)
    c24 = along_x(pair, 2)
    state, p6 = together(state, p6)

    b6 = along_x(p6, 1)
    c6 = along_x(p6, 2)
    b24, c24 = together(b24, c24)

    sent = [
        b24,
        jnp.where(bit[1] == 1, p2, c24[:SLOT]),
        jnp.where(bit[2] == 1, p4, c24[SLOT:]),
    ]
    sent = jnp.concatenate(sent)
    near35 = exchange(sent, 1)
    b6, c6, sent = together(b6, c6, sent)

    near7 = exchange(jnp.concatenate([b6, jnp.where(bit[2] == 1, p6, c6)]), 1)
    state = attend_more(
        state,
        q,
        own,
        [p4, p2, b0, c0, near1, b24, c24, p6, b6, c6],
        [bit[2], bit[1]] + [one] * 8 + [bit[2]] + [one] * 2,
    )
    arrays = [p2, p4, b0, c0, near1, b24, c24, p6, near35, b6, c6, near7]
    ok = [bit[1], bit[2]] + [one] * 8 + [bit[2]] + [one] * 8
    return attend_last(state, q, own, [near35, near7], [one] * 6, arrays, ok)


def solution(mesh):
    return jax.shard_map(
        per_device,
        mesh=mesh,
        in_specs=(
            P(("dp", "ctx"), "tp"),
            P(("dp", "ctx"), "tp"),
            P(("dp", "ctx"), "tp"),
            P(("dp", "ctx")),
        ),
        out_specs=P(("dp", "ctx"), "tp"),
        check_vma=False,
    )
```
